128 devices in a mesh: seq: 16 (over y, z), frame: 8 (over x, core).
Axes of the slice: x: 4, y: 4, z: 4, core: 2. Of those that a mesh axis runs over, the one named last changes fastest.
Arguments:
- patches: bfloat16 [6144, 1280], P('frame'), may hold values from -4 to 4
- vit_gain: float32 [1280], replicated, may hold values from 0.5 to 1.5
- vision_qkv: bfloat16 [1280, 3840], P(None, 'seq')
- vision_out: bfloat16 [1280, 1280], P('seq'), may hold values from -0.15625 to 0.15625
- video_ids: int32 [1536], replicated, may hold values from 0 to 2, never falling along the last dimension, each value on 1 to 960 neighbouring positions
- merge_gain: float32 [1280], replicated, may hold values from 0.5 to 1.5
- merge_up: bfloat16 [5120, 5120], P(None, 'seq'), may hold values from -0.078125 to 0.078125
- merge_down: bfloat16 [5120, 8192], P('seq')
- vision_pos: int32 [1536], replicated, may hold values from 0 to 8191, as said below
- text_embed: bfloat16 [8192, 8192], P(('seq', 'frame')), may hold values from -6 to 6
- llm_gain: float32 [8192], replicated, may hold values from 0.5 to 1.5
- query_weight: bfloat16 [8192, 4096], P(None, 'frame')
- keyvalue_weight: bfloat16 [8192, 2048], P(None, 'frame')
Outputs:
- context: bfloat16 [8192, 4096], P('seq', 'frame')
The draws below stay inside these ranges and needn't reach their ends.
Inputs may be any that keep to these rules, and one draw needn't show every extreme that they name: `vision_pos`: distinct positions. Of the tokens in rows f * 192 to (f + 1) * 192 - 1, for any f, at most 18 lie in one block of 512 positions that starts at a multiple of 512; some block holds exactly 18 of them for every f. `video_ids`: the tokens of one video are consecutive rows.
All inputs are finite; a program needn't handle non-finite values.
Results may differ from the reference program's by a relative error of at most 0.02.
Values may be sent and summed in bfloat16 or wider, within the bound.
No kernel may reach another device: no remote copies, remote signals or barrier semaphores. Data moves between devices by JAX's collectives and lax.ppermute only.
A program may use at most 128 MiB of HBM per device.

```python
import math
import jax
import jax.numpy as jnp
import numpy as np
from jax import lax

VIT_HEADS = 16
VIT_HDIM = 80
D_VIT = 1280
MRG_HID = 5120
D = 8192
HDIM = 128
QPK = 4
KV_HEADS = 8
VIS_DEV = 192
SEQ_DEV = 512
VIS = 1536
PATCHES = 6144
D_MRG = 5120
SEQ = 8192


def draw_vision_qkv(key, part):
    base = jax.random.normal(jax.random.fold_in(key, 3), (D_VIT, VIT_HEADS, 3, VIT_HDIM), jnp.float32) * D_VIT ** (-0.5)
    lifted = base * jnp.array([1.6, 1.6, 1.0], jnp.float32)[None, None, :, None]
    return lifted.reshape(D_VIT, VIT_HEADS * 3 * VIT_HDIM).astype(jnp.bfloat16)


def draw_merge_down(key, part):
    base = jax.random.normal(jax.random.fold_in(key, 41), (MRG_HID, D), jnp.float32) * MRG_HID ** (-0.5)
    direction = jax.random.normal(jax.random.fold_in(key, 42), (D,), jnp.float32)
    lift = 3.0 / MRG_HID
    return (base + lift * direction[None, :]).astype(jnp.bfloat16)


def language_weights(key):
    query_part = jax.random.normal(jax.random.fold_in(key, 21), (D, KV_HEADS, QPK, HDIM), jnp.float32) * (1.6 * D ** (-0.5))
    pair_part = jax.random.normal(jax.random.fold_in(key, 22), (D, KV_HEADS, 2, HDIM), jnp.float32) * D ** (-0.5)
    pair_part = pair_part * jnp.array([1.6, 1.0], jnp.float32)[None, None, :, None]
    return (query_part, pair_part)


def draw_query_weight(key, part):
    query_part, pair_part = language_weights(key)
    return query_part.reshape(D, KV_HEADS * QPK * HDIM).astype(jnp.bfloat16)


def draw_keyvalue_weight(key, part):
    query_part, pair_part = language_weights(key)
    return pair_part.reshape(D, KV_HEADS * 2 * HDIM).astype(jnp.bfloat16)


def draw_vision_pos(key, part):
    frame_total = VIS // VIS_DEV
    block_total = SEQ // SEQ_DEV
    share = VIS_DEV // (2 * block_total)
    order_key = jax.random.fold_in(key, 31)
    place_key = jax.random.fold_in(key, 32)
    hot_block = jax.random.randint(jax.random.fold_in(key, 33), (), 0, block_total).astype(jnp.int32)
    ranking = jax.vmap(lambda single: jax.random.permutation(single, block_total))(jax.random.split(order_key, frame_total)).astype(jnp.int32)
    block_ids = jnp.arange(block_total, dtype=jnp.int32)[None, :]
    hot_rank = jnp.sum(jnp.where(block_ids == hot_block, ranking, 0), axis=1, keepdims=True)
    ranking = jnp.where(block_ids == hot_block, 0, jnp.where(ranking == 0, hot_rank, ranking))
    counts = jnp.where(ranking < block_total // 2, 3 * share, share).astype(jnp.int32)
    block_ends = jnp.cumsum(counts, axis=1)
    block_starts = block_ends - counts
    token_ids = jnp.arange(VIS_DEV, dtype=jnp.int32)
    chosen = jnp.sum((block_ends[:, None, :] <= token_ids[None, :, None]).astype(jnp.int32), axis=2)
    within_own = token_ids[None, :] - jnp.take_along_axis(block_starts, chosen, axis=1)
    earlier = jnp.cumsum(counts, axis=0) - counts
    within = jnp.take_along_axis(earlier, chosen, axis=1) + within_own
    layout = jax.vmap(lambda single: jax.random.permutation(single, SEQ_DEV))(jax.random.split(place_key, block_total)).astype(jnp.int32)
    spots = layout[chosen, within]
    return (chosen * SEQ_DEV + spots).reshape(VIS).astype(jnp.int32)


def shard_levels(stream_key, extent, cuts, low, high):
    def one(axis_at, parts):
        heights = jax.random.uniform(jax.random.fold_in(jax.random.fold_in(stream_key, 6), axis_at), (parts,), jnp.float32, low / len(cuts), high / len(cuts))
        return jnp.repeat(jnp.exp(heights), extent[axis_at] // parts).reshape((-1,) + (1,) * (len(extent) - axis_at - 1))

    level = one(*cuts[0])
    for cut in cuts[1:]:
        level = level * one(*cut)
    return level


def length_profile(number_of, total, limit, slope):
    loads = [(1 << 20) // math.isqrt(grade ** slope) + 1 for grade in range(2, number_of + 1)]
    rest, given = total - limit - (number_of - 1), [1] * (number_of - 1)
    while rest > 0:
        candidates = [i for i in range(number_of - 1) if given[i] < limit]
        mass, budget = sum([loads[i] for i in candidates]), rest
        for i in candidates:
            addition = min(limit - given[i], max(1, budget * loads[i] // mass), rest)
            given[i] = given[i] + addition
            rest = rest - addition
    return np.array([limit] + given)


def uneven_parts(own_key, count, total, most, skew):
    if count == 2:
        one = jax.random.randint(own_key, (), max(1, total - most), min(most, total - 1) + 1)
        return jnp.stack([one, total - one])
    sizes = jnp.asarray(length_profile(count, total, most, skew), jnp.int32)
    pairs = (count - 1) // 2
    donor, receiver = sizes[1:1 + 2 * pairs:2], sizes[2:2 + 2 * pairs:2]
    slack = jnp.minimum(donor - 1, most - receiver)
    shifted = jax.random.randint(jax.random.fold_in(own_key, 1), (pairs,), 0, 1 << 20) % (slack + 1)
    sizes = sizes.at[1:1 + 2 * pairs:2].set(donor - shifted).at[2:2 + 2 * pairs:2].set(receiver + shifted)
    return sizes[jax.random.permutation(jax.random.fold_in(own_key, 2), count)]


def scatter_about(own_key, extent, width, most, shards=(), kind=jnp.bfloat16):
    loudness = shard_levels(own_key, extent, shards, -0.22, 0.18) if shards else 1.0
    entries = jax.random.normal(own_key, extent, jnp.float32) * width * loudness
    return jnp.minimum(jnp.maximum(entries, -most), most).astype(kind)


def setup_inputs(seed: int = 0) -> dict:
    seeds = jax.random.split(jax.random.key(seed), 14)
    patches = scatter_about(seeds[0], (PATCHES, D_VIT), 0.5, 4.0, ((0, 8),))
    vit_gain = jnp.clip(1.0 + 0.1 * jax.random.normal(seeds[1], (D_VIT,), jnp.float32), 0.5, 1.5)
    vision_qkv = draw_vision_qkv(jax.random.fold_in(seeds[13], 71), 0)
    vision_out = scatter_about(seeds[3], (D_VIT, D_VIT), D_VIT ** -0.5, 0.15625, ((0, 16),))
    video_ids = jnp.searchsorted(jnp.cumsum(uneven_parts(seeds[4], 3, VIS, 5 * VIS // 8, 0)), jnp.arange(VIS), side="right").astype(jnp.int32)
    merge_gain = jnp.clip(1.0 + 0.1 * jax.random.normal(seeds[5], (D_VIT,), jnp.float32), 0.5, 1.5)
    merge_up = scatter_about(seeds[6], (D_MRG, MRG_HID), D_MRG ** -0.5, 0.078125, ((1, 16),))
    merge_down = draw_merge_down(jax.random.fold_in(seeds[13], 71), 0)
    vision_pos = draw_vision_pos(jax.random.fold_in(seeds[13], 71), 0)
    text_embed = scatter_about(seeds[9], (SEQ, D), 1.0, 6.0, ((0, 128),))
    llm_gain = jnp.clip(1.0 + 0.1 * jax.random.normal(seeds[10], (D,), jnp.float32), 0.5, 1.5)
    query_weight = draw_query_weight(jax.random.fold_in(seeds[13], 71), 0)
    keyvalue_weight = draw_keyvalue_weight(jax.random.fold_in(seeds[13], 71), 0)
    return dict(patches=patches, vit_gain=vit_gain, vision_qkv=vision_qkv, vision_out=vision_out, video_ids=video_ids, merge_gain=merge_gain, merge_up=merge_up, merge_down=merge_down, vision_pos=vision_pos, text_embed=text_embed, llm_gain=llm_gain, query_weight=query_weight, keyvalue_weight=keyvalue_weight)


epsilon = 1e-06
rope_base = 1000000.0

def rms_scale(matrix, scales):
    widened = matrix.astype(jnp.float32)
    factor = lax.rsqrt(lax.optimization_barrier(jnp.mean(widened * widened, axis=-1, keepdims=True)) + epsilon)
    return widened * factor * scales

def rotary(tensor, positions):
    head_width = tensor.shape[-1]
    half_width = head_width // 2
    inverse = rope_base ** (-2.0 * jnp.arange(half_width, dtype=jnp.float32) / head_width)
    angles = positions.astype(jnp.float32)[:, None] * inverse[None, :]
    cosine = jnp.cos(angles)[:, None, :]
    sine_part = jnp.sin(angles)[:, None, :]
    first_half = tensor[..., :half_width]
    second_half = tensor[..., half_width:]
    return jnp.concatenate([first_half * cosine - second_half * sine_part, second_half * cosine + first_half * sine_part], axis=-1)

def attend_all(queries, key_rows, value_rows, allowed, score_scale):
    scores = jnp.dot(queries, key_rows.T, preferred_element_type=jnp.float32) * score_scale
    scores = jnp.where(allowed, scores, -jnp.inf)
    highest = lax.optimization_barrier(jnp.max(scores, axis=1, keepdims=True))
    weights = jnp.exp(scores - highest)
    row_sum = lax.optimization_barrier(jnp.sum(weights, axis=1, keepdims=True))
    mixed = jnp.dot(weights.astype(jnp.bfloat16), value_rows, preferred_element_type=jnp.float32)
    return mixed / row_sum

def reference(patches, vit_gain, vision_qkv, vision_out, video_ids, merge_gain, merge_up, merge_down, vision_pos, text_embed, llm_gain, query_weight, keyvalue_weight):
    normed_patches = rms_scale(patches, vit_gain).astype(jnp.bfloat16)
    projected = jnp.dot(normed_patches, vision_qkv, preferred_element_type=jnp.float32).astype(jnp.bfloat16)
    projected = projected.reshape(PATCHES, VIT_HEADS, 3, VIT_HDIM)
    stacked = jnp.transpose(projected, (2, 1, 0, 3))
    patch_video = jnp.repeat(video_ids, 4)
    same_video = patch_video[:, None] == patch_video[None, :]
    vit_heads_out = lax.map(lambda triple: attend_all(triple[0], triple[1], triple[2], same_video, VIT_HDIM ** (-0.5)), (stacked[0], stacked[1], stacked[2]))
    vit_context = jnp.transpose(vit_heads_out, (1, 0, 2)).reshape(PATCHES, D_VIT).astype(jnp.bfloat16)
    vit_output = patches.astype(jnp.float32) + jnp.dot(vit_context, vision_out, preferred_element_type=jnp.float32)
    merged_input = rms_scale(vit_output, merge_gain).astype(jnp.bfloat16).reshape(VIS, 4 * D_VIT)
    merge_hidden = jax.nn.gelu(jnp.dot(merged_input, merge_up, preferred_element_type=jnp.float32), approximate=False).astype(jnp.bfloat16)
    vision = jnp.dot(merge_hidden, merge_down, preferred_element_type=jnp.float32).astype(jnp.bfloat16)
    embedded = text_embed.at[vision_pos].set(vision)
    normed_tokens = rms_scale(embedded, llm_gain).astype(jnp.bfloat16)
    positions = jnp.arange(SEQ, dtype=jnp.int32)
    query_full = jnp.dot(normed_tokens, query_weight, preferred_element_type=jnp.float32).reshape(SEQ, KV_HEADS * QPK, HDIM)
    llm_query = rotary(query_full, positions).astype(jnp.bfloat16)
    pair_full = jnp.dot(normed_tokens, keyvalue_weight, preferred_element_type=jnp.float32).reshape(SEQ, KV_HEADS, 2, HDIM)
    llm_keys = rotary(pair_full[:, :, 0], positions).astype(jnp.bfloat16)
    llm_values = pair_full[:, :, 1].astype(jnp.bfloat16)
    causal = positions[:, None] >= positions[None, :]
    key_heads = jnp.repeat(jnp.transpose(llm_keys, (1, 0, 2)), QPK, axis=0)
    value_heads = jnp.repeat(jnp.transpose(llm_values, (1, 0, 2)), QPK, axis=0)
    llm_heads_out = lax.map(lambda triple: attend_all(triple[0], triple[1], triple[2], causal, HDIM ** (-0.5)), (jnp.transpose(llm_query, (1, 0, 2)), key_heads, value_heads))
    return jnp.transpose(llm_heads_out, (1, 0, 2)).reshape(SEQ, KV_HEADS * QPK * HDIM).astype(jnp.bfloat16)
```

```python
import functools
import math

import jax
import jax.numpy as jnp
from jax import lax
from jax.experimental import pallas as pl
from jax.experimental.pallas import tpu as pltpu
from jax.sharding import PartitionSpec as P

VIT_HDIM = 80
HDIM = 128
SIDE = 4
CORES = 2

epsilon = 1e-06
rope_base = 1000000.0
lowest = -1e30
log2e = math.log2(math.e)
bf16 = jnp.bfloat16
f32 = jnp.float32
vmem_limit = 56 * 1024 * 1024


def dot(a, b, contract=((1,), (0,))):
    return lax.dot_general(a, b, (contract, ((), ())), preferred_element_type=f32)


def moved(value, way, step):
    if way == "z":
        pairs = [(i, i - i % SIDE + (i + step) % SIDE) for i in range(SIDE * SIDE)]
    elif way == "y":
        pairs = [(i, (i + SIDE * step) % (SIDE * SIDE)) for i in range(SIDE * SIDE)]
    elif way == "x":
        pairs = [(i, (i + CORES * step) % (CORES * SIDE)) for i in range(CORES * SIDE)]
    else:
        pairs = [(i, i ^ 1) for i in range(CORES * SIDE)]
    return lax.ppermute(value, "seq" if way in "zy" else "frame", pairs)


def ring_gather(value, way):
    return jnp.concatenate([value] + [moved(value, way, d) for d in range(1, SIDE)], axis=0)


def seq_gather(value, first, second):
    stack = ring_gather(value, first)
    return [stack] + [moved(stack, second, d) for d in range(1, SIDE)]


def ring_sum(parts, way):
    arrived = [moved(parts[d], way, d) for d in range(1, SIDE)]
    total = parts[0].astype(f32)
    for a in arrived:
        total = total + a.astype(f32)
    return total.astype(bf16)


def rms_scale(matrix, scales):
    widened = matrix.astype(f32)
    factor = lax.rsqrt(jnp.mean(widened * widened, axis=-1, keepdims=True) + epsilon)
    return widened * factor * scales


def flash_step(key, query_t, value_t, state, scale, allowed):
    highest, total, mixed = state
    scores = dot(key, query_t)
    if allowed is not None:
        scores = jnp.where(allowed, scores, lowest)
    new = jnp.maximum(highest, jnp.max(scores, axis=0, keepdims=True))
    weights = jnp.exp2((scores - new) * scale)
    shrink = jnp.exp2((highest - new) * scale)
    total = total * shrink + jnp.sum(weights, axis=0, keepdims=True)
    mixed = mixed * shrink + dot(value_t, weights.astype(bf16))
    return new, total, mixed


def vit_kernel(rows, bounds, q_ref, kv_ref, *refs, first, last, tile):
    if first:
        refs = (None, None, None) + refs
    m_in, l_in, a_in = refs[:3]
    outs, (m_s, l_s, a_s) = refs[3:-3], refs[-3:]
    lower, upper, frame, x_at, core = (bounds[i] for i in range(5))
    total_rows = rows * CORES * SIDE
    if first:
        m_s[...] = jnp.full(m_s.shape, lowest, f32)
        l_s[...] = jnp.zeros(l_s.shape, f32)
        a_s[...] = jnp.zeros(a_s.shape, f32)
    else:
        m_s[...], l_s[...], a_s[...] = m_in[...], l_in[...], a_in[...]

    def span(at):
        start = jnp.where(at >= upper, upper, jnp.where(at >= lower, lower, 0))
        end = jnp.where(at < lower, lower, jnp.where(at < upper, upper, total_rows))
        return start, end

    first_start, first_end = span(frame * rows)
    last_start, last_end = span(frame * rows + rows - 1)

    def piece(d, _):
        base = (((x_at - d + SIDE) % SIDE) * CORES + core) * rows

        def attend(masked):
            row_at = pl.multiple_of(d * 2 * VIT_HDIM, 2 * VIT_HDIM)
            key = kv_ref[pl.ds(row_at, VIT_HDIM), :].T
            value_t = kv_ref[pl.ds(row_at + VIT_HDIM, VIT_HDIM), :]
            for t in range(rows // tile):
                cut = slice(t * tile, (t + 1) * tile)
                allowed = None
                if masked:
                    at = frame * rows + t * tile + lax.broadcasted_iota(jnp.int32, (1, tile), 1)
                    start, end = span(at)
                    key_at = base + lax.broadcasted_iota(jnp.int32, (rows, 1), 0)
                    allowed = (key_at >= start) & (key_at < end)
                new = flash_step(
                    key,
                    q_ref[:, cut],
                    value_t,
                    (m_s[:, cut], l_s[:, cut], a_s[:, cut]),
                    VIT_HDIM**-0.5 * log2e,
                    allowed,
                )
                m_s[:, cut], l_s[:, cut], a_s[:, cut] = new

        live = (base < last_end) & (base + rows > first_start)
        whole = (base >= last_start) & (base + rows <= first_end)
        pl.when(live & whole)(lambda: attend(False))
        pl.when(live & jnp.logical_not(whole))(lambda: attend(True))
        return 0

    lax.fori_loop(0, SIDE, piece, 0)
    if last:
        result = (a_s[...] / l_s[...]).astype(bf16)
        half = rows // 2
        outs[0][...] = result[:, :half]
        outs[1][...] = result[:, half:]
    else:
        outs[0][...], outs[1][...], outs[2][...] = m_s[...], l_s[...], a_s[...]


def vit_attention(bounds, query_t, pairs, state, last):
    width, rows = query_t.shape
    shapes = [(1, rows), (1, rows), (width, rows)]
    whole = pl.BlockSpec(memory_space=pltpu.VMEM)
    outs = [((width, rows // 2), bf16)] * 2 if last else [(s, f32) for s in shapes]
    inputs = [query_t, pairs] + list(state or [])
    return pl.pallas_call(
        functools.partial(
            vit_kernel, rows, first=state is None, last=last, tile=math.gcd(rows, 256)
        ),
        out_shape=[jax.ShapeDtypeStruct(*o) for o in outs],
        in_specs=[pl.BlockSpec(memory_space=pltpu.SMEM)] + [whole] * len(inputs),
        out_specs=[whole] * len(outs),
        scratch_shapes=[pltpu.VMEM(s, f32) for s in shapes],
        compiler_params=pltpu.CompilerParams(vmem_limit_bytes=vmem_limit),
        cost_estimate=pl.CostEstimate(
            flops=16 * rows * rows * width * 2, bytes_accessed=4 * rows * rows, transcendentals=0
        ),
    )(bounds, *inputs)


def merger_kernel(*refs, rows, side):
    ctx_z, ctx_y, out_z, out_y = refs[0:4], refs[4:8], refs[8:12], refs[12:16]
    patches, gain, up, down, sel_z, sel_y = refs[16:22]
    parts = refs[22:30]
    ctx, proj, up_v, down_v, normed, sems = refs[30:]
    half = rows // 2
    wide = proj.shape[1] // 2
    head = VIT_HDIM
    copies = []
    for pieces_z, pieces_y, target, cut in ((ctx_z, ctx_y, ctx, half), (out_z, out_y, proj, wide)):
        for i in range(side):
            at = i * side * head
            copies.append((pieces_z[i], target.at[pl.ds(at, side * head), pl.ds(0, cut)]))
            for j in range(side):
                at = (j * side + i) * head
                copies.append(
                    (
                        pieces_y[i].at[pl.ds(j * head, head), :],
                        target.at[pl.ds(at, head), pl.ds(cut, cut)],
                    )
                )
    copies += [(up, up_v), (down, down_v)]
    started = [pltpu.make_async_copy(a, b, sems.at[i]) for i, (a, b) in enumerate(copies)]
    for c in started:
        c.start()
    for c in started[:-2]:
        c.wait()
    step = math.gcd(rows, 256)
    for t in range(rows // step):
        cut = slice(t * step, (t + 1) * step)
        out = patches[cut, :].astype(f32) + dot(ctx[:, cut], proj[...], ((0,), (0,)))
        factor = lax.rsqrt(jnp.mean(out * out, axis=1, keepdims=True) + epsilon)
        scaled = out * factor * gain[...]
        for b in range(normed.shape[0]):
            normed[b, cut, :] = scaled[:, b * HDIM : (b + 1) * HDIM]
    started[-2].wait()
    tokens, width = rows // 4, proj.shape[1]
    hidden = jnp.zeros((tokens, up_v.shape[1]), f32)
    for r in range(4):
        line = jnp.concatenate(
            [
                normed[b, pl.ds(r, tokens, stride=4), :].astype(bf16)
                for b in range(normed.shape[0])
            ],
            axis=1,
        )
        hidden = hidden + dot(line, up_v[r * width : (r + 1) * width, :])
    hidden = (0.5 * hidden * (1.0 + lax.erf(hidden * math.sqrt(0.5)))).astype(bf16)
    started[-1].wait()
    columns = down_v.shape[1] // 2
    block = math.gcd(columns, 1024)
    for n, sel in enumerate((sel_z, sel_y)):
        for d in range(side):
            mine = dot(sel[d], hidden).astype(bf16)
            for b in range(columns // block):
                at = n * columns + b * block
                parts[n * side + d][:, b * block : (b + 1) * block] = dot(
                    mine, down_v[:, at : at + block]
                ).astype(bf16)


def merger(ctx_z, ctx_y, out_z, out_y, patches, gain, up, down, sel_z, sel_y):
    rows, width = patches.shape
    whole, far = pl.BlockSpec(memory_space=pltpu.VMEM), pl.BlockSpec(memory_space=pl.ANY)
    side, taken = sel_z.shape[:2]
    part = jax.ShapeDtypeStruct((taken, down.shape[1] // 2), bf16)
    n_copies = 2 * (side + side * side) + 2
    return pl.pallas_call(
        functools.partial(merger_kernel, rows=rows, side=side),
        out_shape=[part] * (2 * side),
        in_specs=[far] * 16 + [whole, whole, far, far, whole, whole],
        out_specs=[whole] * (2 * side),
        scratch_shapes=[
            pltpu.VMEM((side * side * VIT_HDIM, rows), bf16),
            pltpu.VMEM((side * side * VIT_HDIM, width), bf16),
            pltpu.VMEM(up.shape, bf16),
            pltpu.VMEM(down.shape, bf16),
            pltpu.VMEM((width // HDIM, rows, HDIM), f32),
            pltpu.SemaphoreType.DMA((n_copies,)),
        ],
        compiler_params=pltpu.CompilerParams(vmem_limit_bytes=vmem_limit),
        cost_estimate=pl.CostEstimate(
            flops=2 * rows * width * width * 3, bytes_accessed=20 * 1024 * 1024, transcendentals=0
        ),
    )(*ctx_z, *ctx_y, *out_z, *out_y, patches, gain, up, down, sel_z, sel_y)


def project_kernel(x_ref, gain, wq, wkv, cos, sin, *refs, steps, combine):
    if combine:
        texts, where_ref = refs[0:2], refs[2]
        q_out, k_out, v_out = refs[3:6]
    else:
        (out_ref,) = refs[:1]
    acc, factor = refs[-2:]
    step = pl.program_id(0)
    part = x_ref.shape[1] // steps

    @pl.when(step == 0)
    def _():
        squares = jnp.zeros((x_ref.shape[0], 1), f32)
        for i in range(steps):
            piece = x_ref[:, i * part : (i + 1) * part].astype(f32)
            squares = squares + jnp.sum(piece * piece, axis=1, keepdims=True)
        factor[...] = lax.rsqrt(squares / x_ref.shape[1] + epsilon)
        acc[...] = jnp.zeros(acc.shape, f32)

    mine = x_ref[:, pl.ds(pl.multiple_of(step * part, part), part)].astype(f32)
    mine = (mine * factor[...] * gain[...]).astype(bf16)
    n_query = wq.shape[1]
    acc[:, :n_query] += dot(mine, wq[...])
    acc[:, n_query:] += dot(mine, wkv[...])

    @pl.when(step == steps - 1)
    def _():
        heads = n_query // HDIM + 1
        turned = []
        for h in range(heads):
            raw = acc[:, h * HDIM : (h + 1) * HDIM]
            turned.append(
                (raw * cos[...] + pltpu.roll(raw, HDIM // 2, 1) * sin[...]).astype(bf16)
            )
        turned.append(acc[:, heads * HDIM :].astype(bf16))
        done = jnp.concatenate(turned, axis=1)
        if not combine:
            out_ref[...] = done
        else:
            every = jnp.concatenate([texts[0][...], texts[1][...], done], axis=0)
            place = where_ref[...]
            over = ((0,), (0,))
            for h in range(heads - 1):
                q_out[h] = dot(every[:, h * HDIM : (h + 1) * HDIM], place, over).astype(bf16)
            key = every[:, (heads - 1) * HDIM : heads * HDIM]
            k_out[...] = dot(place, key, over).astype(bf16)
            v_out[...] = dot(every[:, heads * HDIM :], place, over).astype(bf16)


def project(x, gain, wq, wkv, cos, sin, combine=None):
    rows, width = x.shape
    steps = 8
    part = width // steps
    n_out = wq.shape[1] + wkv.shape[1]

    def full(a):
        return pl.BlockSpec(a.shape, lambda i: (0,) * a.ndim)

    extra = []
    if combine is None:
        outs = jax.ShapeDtypeStruct((rows, n_out), bf16)
        out_specs = pl.BlockSpec((rows, n_out), lambda i: (0, 0))
    else:
        extra = list(combine)
        block = combine[2].shape[1]
        heads = wq.shape[1] // HDIM
        outs = [
            jax.ShapeDtypeStruct((heads, HDIM, block), bf16),
            jax.ShapeDtypeStruct((block, HDIM), bf16),
            jax.ShapeDtypeStruct((HDIM, block), bf16),
        ]
        out_specs = [
            pl.BlockSpec((heads, HDIM, block), lambda i: (0, 0, 0)),
            pl.BlockSpec((block, HDIM), lambda i: (0, 0)),
            pl.BlockSpec((HDIM, block), lambda i: (0, 0)),
        ]
    return pl.pallas_call(
        functools.partial(project_kernel, steps=steps, combine=combine is not None),
        grid=(steps,),
        out_shape=outs,
        in_specs=[
            full(x),
            pl.BlockSpec((1, part), lambda i: (0, i)),
            pl.BlockSpec((part, wq.shape[1]), lambda i: (i, 0)),
            pl.BlockSpec((part, wkv.shape[1]), lambda i: (i, 0)),
            full(cos),
            full(sin),
        ]
        + [full(e) for e in extra],
        out_specs=out_specs,
        scratch_shapes=[pltpu.VMEM((rows, n_out), f32), pltpu.VMEM((rows, 1), f32)],
        compiler_params=pltpu.CompilerParams(vmem_limit_bytes=vmem_limit),
        cost_estimate=pl.CostEstimate(
            flops=2 * rows * width * n_out,
            bytes_accessed=2 * width * (rows + n_out),
            transcendentals=0,
        ),
    )(x, gain, wq, wkv, cos, sin, *extra)


def llm_kernel(place, q_ref, *refs, side):
    keys, values = refs[0:side], refs[side : 2 * side]
    out_ref, k_s, v_s, sems = refs[2 * side :]
    heads, _, rows = q_ref.shape
    copies = []
    for i in range(side):
        copies.append(
            pltpu.make_async_copy(keys[i], k_s.at[pl.ds(i * side * rows, side * rows), :], sems.at[i])
        )
        copies.append(
            pltpu.make_async_copy(
                values[i], v_s.at[pl.ds(i * side * HDIM, side * HDIM), :], sems.at[side + i]
            )
        )
    for c in copies:
        c.start()
    for c in copies:
        c.wait()
    y_at, z_at = place[0], place[1]

    def block(other, states, masked):
        dy = (y_at - other // side + side) % side
        dz = (z_at - other % side + side) % side
        key = k_s[pl.ds(pl.multiple_of((dy * side + dz) * rows, rows), rows), :]
        value_t = v_s[pl.ds(pl.multiple_of((dz * side + dy) * HDIM, HDIM), HDIM), :]
        allowed = None
        if masked:
            allowed = lax.broadcasted_iota(jnp.int32, (rows, rows), 0) <= lax.broadcasted_iota(
                jnp.int32, (rows, rows), 1
            )
        return tuple(
            flash_step(key, q_ref[h], value_t, states[h], HDIM**-0.5 * log2e, allowed)
            for h in range(heads)
        )

    empty = (
        jnp.full((1, rows), lowest, f32),
        jnp.zeros((1, rows), f32),
        jnp.zeros((HDIM, rows), f32),
    )
    own = y_at * side + z_at
    states = block(own, (empty,) * heads, True)
    states = lax.fori_loop(0, own, lambda j, s: block(j, s, False), states)
    for h in range(heads):
        _, total, mixed = states[h]
        out_ref[:, h * HDIM : (h + 1) * HDIM] = (mixed / total).T.astype(bf16)


def llm_attention(place, query_t, keys, values):
    side = len(keys)
    heads, _, rows = query_t.shape
    whole, far = pl.BlockSpec(memory_space=pltpu.VMEM), pl.BlockSpec(memory_space=pl.ANY)
    return pl.pallas_call(
        functools.partial(llm_kernel, side=side),
        out_shape=jax.ShapeDtypeStruct((rows, heads * HDIM), bf16),
        in_specs=[pl.BlockSpec(memory_space=pltpu.SMEM), whole] + [far] * (2 * side),
        out_specs=whole,
        scratch_shapes=[
            pltpu.VMEM((side * side * rows, HDIM), bf16),
            pltpu.VMEM((side * side * HDIM, rows), bf16),
            pltpu.SemaphoreType.DMA((2 * side,)),
        ],
        compiler_params=pltpu.CompilerParams(vmem_limit_bytes=vmem_limit),
        cost_estimate=pl.CostEstimate(
            flops=64 * rows * rows * HDIM * heads, bytes_accessed=2**23, transcendentals=0
        ),
    )(place, query_t, *keys, *values)


def rotary_tables(positions):
    half = HDIM // 2
    inverse = rope_base ** (-2.0 * jnp.arange(half, dtype=f32) / HDIM)
    angles = positions.astype(f32)[:, None] * inverse[None, :]
    cosine, sine = jnp.cos(angles), jnp.sin(angles)
    return jnp.concatenate([cosine, cosine], axis=1), jnp.concatenate([-sine, sine], axis=1)


def local(
    patches,
    vit_gain,
    vision_qkv,
    vision_out,
    video_ids,
    merge_gain,
    merge_up,
    merge_down,
    vision_pos,
    text_embed,
    llm_gain,
    query_weight,
    keyvalue_weight,
):
    frame = lax.axis_index("frame").astype(jnp.int32)
    seq = lax.axis_index("seq").astype(jnp.int32)
    x_at, core = frame // CORES, frame % CORES
    y_at, z_at = seq // SIDE, seq % SIDE
    frames, blocks = CORES * SIDE, SIDE * SIDE
    tokens = vision_pos.shape[0] // frames
    seq_block = text_embed.shape[0] * frames
    cap = 3 * tokens // (2 * blocks)
    slot_rows = -(-cap // 8) * 8

    normed = rms_scale(patches, vit_gain).astype(bf16)
    projected = dot(vision_qkv, normed, ((0,), (1,))).astype(bf16)
    vit_query, vit_pairs = projected[:VIT_HDIM], projected[VIT_HDIM:]
    near = ring_gather(vit_pairs, "x")
    away = moved(near, "core", 1)
    text_embed, near = lax.optimization_barrier((text_embed, near))
    counts = [4 * jnp.sum((video_ids < v).astype(jnp.int32)) for v in (1, 2)]
    bounds = jnp.stack(counts + [frame, x_at, core]).astype(jnp.int32)
    bounds_away = jnp.stack(counts + [frame, x_at, 1 - core]).astype(jnp.int32)
    state = vit_attention(bounds, vit_query, near, None, False)
    ctx_z, ctx_y = vit_attention(bounds_away, vit_query, away, state, True)

    wide = vision_out.shape[1] // 2
    out_z = seq_gather(vision_out[:, :wide], "z", "y")
    out_y = seq_gather(vision_out[:, wide:], "y", "z")

    pos = vision_pos.reshape(frames, tokens)
    owner = pos // seq_block
    earlier = jnp.arange(tokens)[:, None] > jnp.arange(tokens)[None, :]
    rank = jnp.sum(
        ((owner[:, :, None] == owner[:, None, :]) & earlier[None]).astype(jnp.int32), axis=2
    )
    own_owner = lax.dynamic_slice_in_dim(owner, frame, 1, 0)[0]
    own_rank = lax.dynamic_slice_in_dim(rank, frame, 1, 0)[0]
    d_at = jnp.arange(SIDE, dtype=jnp.int32)[:, None]
    e_at = (jnp.arange(SIDE * cap, dtype=jnp.int32) // cap)[None, :]
    slot = (jnp.arange(SIDE * cap, dtype=jnp.int32) % cap)[None, :]

    def selector(to_y, to_z):
        block = (to_y % SIDE) * SIDE + to_z % SIDE
        return (
            (own_owner[None, None, :] == block[:, :, None])
            & (own_rank[None, None, :] == slot[:, :, None])
        ).astype(bf16)

    sel_z = selector(y_at + e_at, z_at + d_at)
    sel_y = selector(y_at + d_at, z_at + e_at)

    parts = merger(
        seq_gather(ctx_z, "z", "y"),
        seq_gather(ctx_y, "y", "z"),
        out_z,
        out_y,
        patches,
        merge_gain[None, :],
        merge_up,
        merge_down,
        sel_z,
        sel_y,
    )
    rows = []
    for some, first, second in ((parts[:SIDE], "z", "y"), (parts[SIDE:], "y", "z")):
        total = ring_sum(some, first)
        total = ring_sum([total[e * cap : (e + 1) * cap] for e in range(SIDE)], second)
        total = jnp.pad(total, ((0, slot_rows - cap), (0, 0)))
        stack = ring_gather(total, "x")
        rows.append(jnp.concatenate([stack, moved(stack, "core", 1)], axis=0))
    vision = jnp.concatenate(rows, axis=1)

    back = (x_at - jnp.arange(SIDE, dtype=jnp.int32)) % SIDE
    order = jnp.concatenate([back * CORES + core, back * CORES + 1 - core])
    in_slot = (owner == seq)[:, None, :] & (
        rank[:, None, :] == jnp.arange(slot_rows, dtype=jnp.int32)[None, :, None]
    )
    spot = jnp.sum(jnp.where(in_slot, (pos - seq * seq_block + 1)[:, None, :], 0), axis=2) - 1
    spot = jnp.take(spot, order, axis=0).reshape(-1)
    share = text_embed.shape[0]
    text_spot = (order[:, None] * share + jnp.arange(share, dtype=jnp.int32)[None, :]).reshape(-1)
    line = jnp.arange(seq_block, dtype=jnp.int32)
    place_vision = spot[:, None] == line[None, :]
    place_text = (text_spot[:, None] == line[None, :]) & ~jnp.any(place_vision, axis=0)[None, :]
    place = jnp.concatenate([place_text, place_vision], axis=0).astype(bf16)

    text_near = ring_gather(text_embed, "x")
    text_away = moved(text_near, "core", 1)
    gain = llm_gain[None, :]
    cos, sin = rotary_tables(seq * seq_block + jnp.concatenate([text_spot, spot]))
    texts, at = [], 0
    for t in (text_near, text_away):
        end = at + t.shape[0]
        texts.append(project(t, gain, query_weight, keyvalue_weight, cos[at:end], sin[at:end]))
        at = end
    query_t, key, value_t = project(
        vision, gain, query_weight, keyvalue_weight, cos[at:], sin[at:], (*texts, place)
    )
    keys = seq_gather(key, "z", "y")
    values = seq_gather(value_t, "y", "z")
    return llm_attention(jnp.stack([y_at, z_at]), query_t, keys, values)


def solution(mesh):
    return jax.shard_map(
        local,
        mesh=mesh,
        in_specs=(
            P("frame", None),
            P(),
            P(None, "seq"),
            P("seq", None),
            P(),
            P(),
            P(None, "seq"),
            P("seq", None),
            P(),
            P(("seq", "frame"), None),
            P(),
            P(None, "frame"),
            P(None, "frame"),
        ),
        out_specs=P("seq", "frame"),
        check_vma=False,
    )
```

```python
import functools
import math

import jax
import jax.numpy as jnp
from jax import lax
from jax.experimental import pallas as pl
from jax.experimental.pallas import tpu as pltpu
from jax.sharding import PartitionSpec as P

VIT_HDIM = 80
HDIM = 128
SIDE = 4
CORES = 2

epsilon = 1e-06
rope_base = 1000000.0
lowest = -1e30
log2e = math.log2(math.e)
bf16 = jnp.bfloat16
f32 = jnp.float32
vmem_limit = 56 * 1024 * 1024


def dot(a, b, contract=((1,), (0,))):
    return lax.dot_general(a, b, (contract, ((), ())), preferred_element_type=f32)


def moved(value, way, step):
    if way == "z":
        pairs = [(i, i - i % SIDE + (i + step) % SIDE) for i in range(SIDE * SIDE)]
    elif way == "y":
        pairs = [(i, (i + SIDE * step) % (SIDE * SIDE)) for i in range(SIDE * SIDE)]
    elif way == "x":
        pairs = [(i, (i + CORES * step) % (CORES * SIDE)) for i in range(CORES * SIDE)]
    else:
        pairs = [(i, i ^ 1) for i in range(CORES * SIDE)]
    return lax.ppermute(value, "seq" if way in "zy" else "frame", pairs)


def after(values, *others):
    return lax.optimization_barrier((values, others))[0]


def ring_gather(value, way):
    return jnp.concatenate([value] + [moved(value, way, d) for d in range(1, SIDE)], axis=0)


def ring_sum(parts, way):
    arrived = [moved(parts[d], way, d) for d in range(1, SIDE)]
    total = parts[0].astype(f32)
    for a in arrived:
        total = total + a.astype(f32)
    return total.astype(bf16)


def rms_scale(matrix, scales):
    widened = matrix.astype(f32)
    factor = lax.rsqrt(jnp.mean(widened * widened, axis=-1, keepdims=True) + epsilon)
    return widened * factor * scales


def flash_block(query, key, value, over_key, over_value, refs, scale, allowed):
    m_ref, l_ref, a_ref = refs
    scores = dot(query, key, ((1,), (over_key,)))
    if allowed is not None:
        scores = jnp.where(allowed, scores, lowest)
    lanes = [slice(i * HDIM, (i + 1) * HDIM) for i in range(scores.shape[1] // HDIM)]
    top = scores[:, lanes[0]]
    for lane in lanes[1:]:
        top = jnp.maximum(top, scores[:, lane])
    old = m_ref[...]
    new = jnp.maximum(old, jnp.max(top, axis=1, keepdims=True))
    shrink = jnp.exp2((old - new) * scale)
    total, weights = l_ref[...] * shrink, []
    for lane in lanes:
        part = jnp.exp2((scores[:, lane] - new) * scale)
        total = total + part
        weights.append(part.astype(bf16))
    mixed = dot(jnp.concatenate(weights, axis=1), value, ((1,), (over_value,)))
    a_ref[...] = a_ref[...] * shrink[:, : mixed.shape[1]] + mixed
    l_ref[...] = total
    m_ref[...] = new


def flash_start(refs):
    refs[0][...] = jnp.full(refs[0].shape, lowest, f32)
    refs[1][...] = jnp.zeros(refs[1].shape, f32)
    refs[2][...] = jnp.zeros(refs[2].shape, f32)


def flash_end(refs):
    return refs[2][...] / jnp.sum(refs[1][...], axis=1, keepdims=True)


def vit_kernel(bounds, q_ref, kv_ref, out_ref, q_s, *state):
    rows = q_ref.shape[1]
    pieces = kv_ref.shape[0] // (2 * VIT_HDIM)
    lower, upper, frame = (bounds[i] for i in range(3))
    flash_start(state)
    q_s[...] = q_ref[...].T

    def span(at):
        start = jnp.where(at >= upper, upper, jnp.where(at >= lower, lower, 0))
        end = jnp.where(at < lower, lower, jnp.where(at < upper, upper, rows * pieces))
        return start, end

    first_start, first_end = span(frame * rows)
    last_start, last_end = span(frame * rows + rows - 1)

    def piece(d, _):
        base = d * rows

        def attend(masked):
            row_at = pl.multiple_of(d * 2 * VIT_HDIM, 2 * VIT_HDIM)
            key_t = kv_ref[pl.ds(row_at, VIT_HDIM), :]
            value = kv_ref[pl.ds(row_at + VIT_HDIM, VIT_HDIM), :].T
            allowed = None
            if masked:
                at = frame * rows + lax.broadcasted_iota(jnp.int32, (rows, 1), 0)
                start, end = span(at)
                key_at = base + lax.broadcasted_iota(jnp.int32, (1, rows), 1)
                allowed = (key_at >= start) & (key_at < end)
            flash_block(q_s[...], key_t, value, 0, 0, state, VIT_HDIM**-0.5 * log2e, allowed)

        live = (base < last_end) & (base + rows > first_start)
        whole = (base >= last_start) & (base + rows <= first_end)
        pl.when(live & whole)(lambda: attend(False))
        pl.when(live & jnp.logical_not(whole))(lambda: attend(True))
        return 0

    lax.fori_loop(0, pieces, piece, 0)
    out_ref[...] = flash_end(state).T.astype(bf16)


def vit_attention(bounds, query_t, pairs):
    width, rows = query_t.shape
    whole = pl.BlockSpec(memory_space=pltpu.VMEM)
    return pl.pallas_call(
        vit_kernel,
        out_shape=jax.ShapeDtypeStruct((width, rows), bf16),
        in_specs=[pl.BlockSpec(memory_space=pltpu.SMEM), whole, whole],
        out_specs=whole,
        scratch_shapes=[pltpu.VMEM((rows, width), bf16)]
        + [pltpu.VMEM(s, f32) for s in ((rows, HDIM), (rows, HDIM), (rows, width))],
        compiler_params=pltpu.CompilerParams(vmem_limit_bytes=vmem_limit),
        cost_estimate=pl.CostEstimate(
            flops=32 * rows * rows * width * 2, bytes_accessed=4 * rows * rows, transcendentals=0
        ),
    )(bounds, query_t, pairs)


def merger_kernel(place, ctx, *refs, rows, side):
    out_w, refs = refs[:CORES], refs[CORES:]
    patches, gain, up, down, sel_z, sel_y = refs[:6]
    parts = refs[6 : 6 + 2 * side]
    proj, up_v, down_v, normed, sems = refs[6 + 2 * side :]
    y_at, z_at, head = place[0], place[1], VIT_HDIM
    copies = []
    for i in range(side):
        for j in range(side):
            at = (((y_at - i + side) % side) * side + (z_at - j + side) % side) * head
            rows_at = pl.ds(pl.multiple_of(at, head), head)
            for c, source in enumerate(out_w):
                wide = source.shape[1]
                columns = pl.multiple_of(((place[2] + c) % CORES) * wide, wide)
                copies.append(
                    (
                        source.at[pl.ds((i * side + j) * head, head), :],
                        proj.at[rows_at, pl.ds(columns, wide)],
                    )
                )
    copies += [(up, up_v), (down, down_v)]
    started = [pltpu.make_async_copy(a, b, sems.at[i]) for i, (a, b) in enumerate(copies)]
    for c in started:
        c.start()
    for c in started[:-2]:
        c.wait()
    step = math.gcd(rows, 256)
    for t in range(rows // step):
        cut = slice(t * step, (t + 1) * step)
        out = patches[cut, :].astype(f32) + dot(ctx[:, cut], proj[...], ((0,), (0,)))
        factor = lax.rsqrt(jnp.mean(out * out, axis=1, keepdims=True) + epsilon)
        scaled = out * factor * gain[...]
        for b in range(normed.shape[0]):
            normed[b, cut, :] = scaled[:, b * HDIM : (b + 1) * HDIM]
    started[-2].wait()
    tokens, width = rows // 4, proj.shape[1]
    hidden = jnp.zeros((tokens, up_v.shape[1]), f32)
    for r in range(4):
        line = jnp.concatenate(
            [
                normed[b, pl.ds(r, tokens, stride=4), :].astype(bf16)
                for b in range(normed.shape[0])
            ],
            axis=1,
        )
        hidden = hidden + dot(line, up_v[r * width : (r + 1) * width, :])
    hidden = (0.5 * hidden * (1.0 + lax.erf(hidden * math.sqrt(0.5)))).astype(bf16)
    started[-1].wait()
    columns = down_v.shape[1] // 2
    block = math.gcd(columns, 1024)
    for n, sel in enumerate((sel_z, sel_y)):
        for d in range(side):
            mine = dot(sel[d], hidden).astype(bf16)
            for b in range(columns // block):
                at = n * columns + b * block
                parts[n * side + d][:, b * block : (b + 1) * block] = dot(
                    mine, down_v[:, at : at + block]
                ).astype(bf16)


def merger(place, ctx, out_w, patches, gain, up, down, sel_z, sel_y):
    rows, width = patches.shape
    whole, far = pl.BlockSpec(memory_space=pltpu.VMEM), pl.BlockSpec(memory_space=pl.ANY)
    side, taken = sel_z.shape[:2]
    part = jax.ShapeDtypeStruct((taken, down.shape[1] // 2), bf16)
    return pl.pallas_call(
        functools.partial(merger_kernel, rows=rows, side=side),
        out_shape=[part] * (2 * side),
        in_specs=[pl.BlockSpec(memory_space=pltpu.SMEM), whole]
        + [far] * CORES
        + [whole, whole, far, far, whole, whole],
        out_specs=[whole] * (2 * side),
        scratch_shapes=[
            pltpu.VMEM(ctx.shape[:1] + (width,), bf16),
            pltpu.VMEM(up.shape, bf16),
            pltpu.VMEM(down.shape, bf16),
            pltpu.VMEM((width // HDIM, rows, HDIM), f32),
            pltpu.SemaphoreType.DMA((side * side * CORES + 2,)),
        ],
        compiler_params=pltpu.CompilerParams(vmem_limit_bytes=vmem_limit),
        cost_estimate=pl.CostEstimate(
            flops=2 * rows * width * width * 3, bytes_accessed=20 * 1024 * 1024, transcendentals=0
        ),
    )(place, ctx, *out_w, patches, gain, up, down, sel_z, sel_y)


def project_kernel(*refs, lots, steps, combine):
    xs, (gain, wq, wkv, cos, sin) = refs[:lots], refs[lots : lots + 5]
    refs = refs[lots + 5 :]
    if combine:
        text, where_ref, q_out, kv_out = refs[:4]
    else:
        out_ref = refs[0]
    acc, factor = refs[-2:]
    step = pl.program_id(0)
    width = xs[0].shape[1]
    part = width // steps
    n_query = wq.shape[1]
    bases = [0]
    for x_ref in xs:
        bases.append(bases[-1] + x_ref.shape[0])

    @pl.when(step == 0)
    def _():
        for x_ref, base in zip(xs, bases):
            squares = jnp.zeros((x_ref.shape[0], HDIM), f32)
            for i in range(width // HDIM):
                piece = x_ref[:, i * HDIM : (i + 1) * HDIM].astype(f32)
                squares = squares + piece * piece
            factor[base : base + x_ref.shape[0], :] = lax.rsqrt(
                jnp.sum(squares, axis=1, keepdims=True) / width + epsilon
            )
        acc[...] = jnp.zeros(acc.shape, f32)

    at = pl.multiple_of(step * part, part)
    mine = jnp.concatenate(
        [
            (
                x_ref[:, pl.ds(at, part)].astype(f32)
                * factor[base : base + x_ref.shape[0], :]
                * gain[...]
            ).astype(bf16)
            for x_ref, base in zip(xs, bases)
        ],
        axis=0,
    )
    acc[:, :n_query] += dot(mine, wq[...])
    acc[:, n_query:] += dot(mine, wkv[...])

    @pl.when(step == steps - 1)
    def _():
        heads = n_query // HDIM + 1
        turned = []
        for h in range(heads):
            raw = acc[:, h * HDIM : (h + 1) * HDIM]
            turned.append(
                (raw * cos[...] + pltpu.roll(raw, HDIM // 2, 1) * sin[...]).astype(bf16)
            )
        turned.append(acc[:, heads * HDIM :].astype(bf16))
        done = jnp.concatenate(turned, axis=1)
        if not combine:
            out_ref[...] = done
        else:
            every = jnp.concatenate([text[...], done], axis=0)
            place = where_ref[...]
            over = ((0,), (0,))
            q_out[...] = dot(place, every[:, :n_query], over).astype(bf16)
            kv_out[...] = dot(place, every[:, n_query:], over).astype(bf16)


def project(xs, gain, wq, wkv, cos, sin, combine=None):
    rows, width = sum(x.shape[0] for x in xs), xs[0].shape[1]
    steps = 8
    part = width // steps
    n_out = wq.shape[1] + wkv.shape[1]

    def full(a):
        return pl.BlockSpec(a.shape, lambda i: (0,) * len(a.shape))

    extra = []
    if combine is None:
        outs = jax.ShapeDtypeStruct((rows, n_out), bf16)
        out_specs = full(outs)
    else:
        extra = list(combine)
        block = combine[1].shape[1]
        outs = [
            jax.ShapeDtypeStruct((block, wq.shape[1]), bf16),
            jax.ShapeDtypeStruct((block, wkv.shape[1]), bf16),
        ]
        out_specs = [full(o) for o in outs]
    return pl.pallas_call(
        functools.partial(
            project_kernel, lots=len(xs), steps=steps, combine=combine is not None
        ),
        grid=(steps,),
        out_shape=outs,
        in_specs=[full(x) for x in xs]
        + [
            pl.BlockSpec((1, part), lambda i: (0, i)),
            pl.BlockSpec((part, wq.shape[1]), lambda i: (i, 0)),
            pl.BlockSpec((part, wkv.shape[1]), lambda i: (i, 0)),
            full(cos),
            full(sin),
        ]
        + [full(e) for e in extra],
        out_specs=out_specs,
        scratch_shapes=[pltpu.VMEM((rows, n_out), f32), pltpu.VMEM((rows, 1), f32)],
        compiler_params=pltpu.CompilerParams(vmem_limit_bytes=vmem_limit),
        cost_estimate=pl.CostEstimate(
            flops=2 * rows * width * n_out,
            bytes_accessed=2 * width * (rows + n_out),
            transcendentals=0,
        ),
    )(*xs, gain, wq, wkv, cos, sin, *extra)


def llm_kernel(place, q_ref, kv_ref, out_ref, q_s, *state):
    rows, heads = q_ref.shape[0], q_ref.shape[1] // HDIM
    step = 2 * rows
    own = place[0]
    flash_start(state)
    for h in range(heads):
        q_s[h * rows : (h + 1) * rows, :] = q_ref[:, h * HDIM : (h + 1) * HDIM]

    def block(j, masked):
        at = pl.ds(pl.multiple_of(j * step, step), step)
        allowed = None
        if masked:
            line = lax.broadcasted_iota(jnp.int32, (heads * rows, 1), 0)
            key_at = j * step + lax.broadcasted_iota(jnp.int32, (1, step), 1)
            allowed = key_at <= own * rows + line % rows
        key, value = kv_ref[at, :HDIM], kv_ref[at, HDIM:]
        flash_block(q_s[...], key, value, 1, 0, state, HDIM**-0.5 * log2e, allowed)

    lax.fori_loop(0, own // 2, lambda j, _: block(j, False), None)
    block(own // 2, True)
    result = flash_end(state).astype(bf16)
    for h in range(heads):
        out_ref[:, h * HDIM : (h + 1) * HDIM] = result[h * rows : (h + 1) * rows, :]


def llm_attention(place, query, pairs):
    rows, width = query.shape
    whole = pl.BlockSpec(memory_space=pltpu.VMEM)
    lines = rows * (width // HDIM)
    return pl.pallas_call(
        llm_kernel,
        out_shape=jax.ShapeDtypeStruct((rows, width), bf16),
        in_specs=[pl.BlockSpec(memory_space=pltpu.SMEM), whole, whole],
        out_specs=whole,
        scratch_shapes=[pltpu.VMEM((lines, HDIM), bf16)] + [pltpu.VMEM((lines, HDIM), f32)] * 3,
        compiler_params=pltpu.CompilerParams(vmem_limit_bytes=vmem_limit),
        cost_estimate=pl.CostEstimate(
            flops=64 * rows * rows * width, bytes_accessed=2**23, transcendentals=0
        ),
    )(place, query, pairs)


def rotary_tables(positions):
    half = HDIM // 2
    inverse = rope_base ** (-2.0 * jnp.arange(half, dtype=f32) / HDIM)
    angles = positions.astype(f32)[:, None] * inverse[None, :]
    cosine, sine = jnp.cos(angles), jnp.sin(angles)
    return jnp.concatenate([cosine, cosine], axis=1), jnp.concatenate([-sine, sine], axis=1)


def local(
    patches,
    vit_gain,
    vision_qkv,
    vision_out,
    video_ids,
    merge_gain,
    merge_up,
    merge_down,
    vision_pos,
    text_embed,
    llm_gain,
    query_weight,
    keyvalue_weight,
):
    frame = lax.axis_index("frame").astype(jnp.int32)
    seq = lax.axis_index("seq").astype(jnp.int32)
    y_at, z_at = seq // SIDE, seq % SIDE
    frames, blocks = CORES * SIDE, SIDE * SIDE
    tokens = vision_pos.shape[0] // frames
    seq_block = text_embed.shape[0] * frames
    cap = 3 * tokens // (2 * blocks)
    slot_rows = -(-cap // 8) * 8

    normed = rms_scale(patches, vit_gain).astype(bf16)
    projected = dot(vision_qkv, normed, ((0,), (1,))).astype(bf16)
    vit_query, vit_pairs = projected[:VIT_HDIM], projected[VIT_HDIM:]
    core = frame % CORES
    wide = vision_out.shape[1] // CORES
    half_out = lax.dynamic_slice_in_dim(vision_out, core * wide, wide, 1)
    ring = ring_gather(half_out, "z")
    out_w = ring_gather(ring, "y")
    out_w = [out_w, moved(out_w, "core", 1)]
    pairs = after(lax.all_gather(vit_pairs, "frame", axis=0, tiled=True), out_w)
    texts = lax.all_gather(after(text_embed, pairs), "frame", axis=0, tiled=True)
    counts = [4 * jnp.sum((video_ids < v).astype(jnp.int32)) for v in (1, 2)]
    bounds = jnp.stack(counts + [frame]).astype(jnp.int32)
    context_t = vit_attention(bounds, vit_query, pairs)

    pos = vision_pos.reshape(frames, tokens)
    owner = pos // seq_block
    earlier = jnp.arange(tokens)[:, None] > jnp.arange(tokens)[None, :]
    rank = jnp.sum(
        ((owner[:, :, None] == owner[:, None, :]) & earlier[None]).astype(jnp.int32), axis=2
    )
    own_owner = lax.dynamic_slice_in_dim(owner, frame, 1, 0)[0]
    own_rank = lax.dynamic_slice_in_dim(rank, frame, 1, 0)[0]
    d_at = jnp.arange(SIDE, dtype=jnp.int32)[:, None]
    e_at = (jnp.arange(SIDE * cap, dtype=jnp.int32) // cap)[None, :]
    slot = (jnp.arange(SIDE * cap, dtype=jnp.int32) % cap)[None, :]

    def selector(to_y, to_z):
        block = (to_y % SIDE) * SIDE + to_z % SIDE
        return (
            (own_owner[None, None, :] == block[:, :, None])
            & (own_rank[None, None, :] == slot[:, :, None])
        ).astype(bf16)

    sel_z = selector(y_at + e_at, z_at + d_at)
    sel_y = selector(y_at + d_at, z_at + e_at)

    in_slot = (owner == seq)[:, None, :] & (
        rank[:, None, :] == jnp.arange(slot_rows, dtype=jnp.int32)[None, :, None]
    )
    spot = jnp.sum(jnp.where(in_slot, (pos - seq * seq_block + 1)[:, None, :], 0), axis=2) - 1
    spot = spot.reshape(-1)
    line = jnp.arange(seq_block, dtype=jnp.int32)
    place_vision = spot[:, None] == line[None, :]
    place_text = (line[:, None] == line[None, :]) & ~jnp.any(place_vision, axis=0)[None, :]
    place = jnp.concatenate([place_text, place_vision], axis=0).astype(bf16)

    gain = llm_gain[None, :]
    cos, sin = rotary_tables(seq * seq_block + jnp.concatenate([line, spot]))
    n_text = seq_block
    weights = (query_weight, keyvalue_weight)

    contexts = jnp.broadcast_to(context_t, (blocks, *context_t.shape))
    contexts = lax.all_to_all(contexts, "seq", split_axis=0, concat_axis=0, tiled=True)
    parts = merger(
        jnp.stack([y_at, z_at, core]),
        contexts.reshape(-1, patches.shape[0]),
        out_w,
        patches,
        merge_gain[None, :],
        merge_up,
        merge_down,
        sel_z,
        sel_y,
    )
    text = project([after(texts, parts)], gain, *weights, cos[:n_text], sin[:n_text])
    rows = []
    for some, first, second in ((parts[:SIDE], "z", "y"), (parts[SIDE:], "y", "z")):
        total = ring_sum(some, first)
        total = ring_sum([total[e * cap : (e + 1) * cap] for e in range(SIDE)], second)
        rows.append(jnp.pad(total, ((0, slot_rows - cap), (0, 0))))
    vision = lax.all_gather(jnp.concatenate(rows, axis=1), "frame", axis=0, tiled=True)

    query, pair = project(
        [vision], gain, *weights, cos[n_text:], sin[n_text:], (text, place)
    )
    llm_pairs = lax.all_gather(pair, "seq", axis=0, tiled=True)
    return llm_attention(seq[None], query, llm_pairs)


def solution(mesh):
    return jax.shard_map(
        local,
        mesh=mesh,
        in_specs=(
            P("frame", None),
            P(),
            P(None, "seq"),
            P("seq", None),
            P(),
            P(),
            P(None, "seq"),
            P("seq", None),
            P(),
            P(("seq", "frame"), None),
            P(),
            P(None, "frame"),
            P(None, "frame"),
        ),
        out_specs=P("seq", "frame"),
        check_vma=False,
    )
```

```python
import functools
import math

import jax
import jax.numpy as jnp
from jax import lax
from jax.experimental import pallas as pl
from jax.experimental.pallas import tpu as pltpu
from jax.sharding import PartitionSpec as P

VIT_HDIM = 80
HDIM = 128
SIDE = 4
CORES = 2

epsilon = 1e-06
rope_base = 1000000.0
lowest = -1e30
log2e = math.log2(math.e)
bf16 = jnp.bfloat16
f32 = jnp.float32
vmem_limit = 56 * 1024 * 1024


def dot(a, b, contract=((1,), (0,))):
    return lax.dot_general(a, b, (contract, ((), ())), preferred_element_type=f32)


def moved(value, way, step):
    if way == "z":
        pairs = [(i, i - i % SIDE + (i + step) % SIDE) for i in range(SIDE * SIDE)]
    elif way == "y":
        pairs = [(i, (i + SIDE * step) % (SIDE * SIDE)) for i in range(SIDE * SIDE)]
    elif way == "x":
        pairs = [(i, (i + CORES * step) % (CORES * SIDE)) for i in range(CORES * SIDE)]
    else:
        pairs = [(i, i ^ 1) for i in range(CORES * SIDE)]
    return lax.ppermute(value, "seq" if way in "zy" else "frame", pairs)


def after(values, *others):
    return lax.optimization_barrier((values, others))[0]


def sent_to_all(value):
    copies = jnp.broadcast_to(value, (SIDE * SIDE, *value.shape))
    return lax.all_to_all(copies, "seq", split_axis=0, concat_axis=0, tiled=True)


def ring_gather(value, way):
    return jnp.concatenate([value] + [moved(value, way, d) for d in range(1, SIDE)], axis=0)


def ring_sum(parts, way, *others):
    arrived = [moved(parts[d], way, d) for d in range(1, SIDE)]
    if others:
        arrived = after(arrived, *others)
    total = parts[0].astype(f32)
    for a in arrived:
        total = total + a.astype(f32)
    return total.astype(bf16)


def rms_scale(matrix, scales):
    widened = matrix.astype(f32)
    factor = lax.rsqrt(jnp.mean(widened * widened, axis=-1, keepdims=True) + epsilon)
    return widened * factor * scales


def flash_block(query, key, value, over_key, over_value, refs, scale, allowed):
    m_ref, l_ref, a_ref = refs
    scores = dot(query, key, ((1,), (over_key,)))
    if allowed is not None:
        scores = jnp.where(allowed, scores, lowest)
    lanes = [slice(i * HDIM, (i + 1) * HDIM) for i in range(scores.shape[1] // HDIM)]
    top = scores[:, lanes[0]]
    for lane in lanes[1:]:
        top = jnp.maximum(top, scores[:, lane])
    old = m_ref[...]
    new = jnp.maximum(old, jnp.max(top, axis=1, keepdims=True))
    shrink = jnp.exp2((old - new) * scale)
    total, weights = l_ref[...] * shrink, []
    for lane in lanes:
        part = jnp.exp2((scores[:, lane] - new) * scale)
        total = total + part
        weights.append(part.astype(bf16))
    mixed = dot(jnp.concatenate(weights, axis=1), value, ((1,), (over_value,)))
    a_ref[...] = a_ref[...] * shrink[:, : mixed.shape[1]] + mixed
    l_ref[...] = total
    m_ref[...] = new


def flash_start(refs):
    refs[0][...] = jnp.full(refs[0].shape, lowest, f32)
    refs[1][...] = jnp.zeros(refs[1].shape, f32)
    refs[2][...] = jnp.zeros(refs[2].shape, f32)


def flash_end(refs):
    return refs[2][...] / jnp.sum(refs[1][...], axis=1, keepdims=True)


def vit_kernel(bounds, q_ref, kv_ref, out_ref, q_s, *state):
    rows = q_ref.shape[1]
    pieces = kv_ref.shape[0] // (2 * VIT_HDIM)
    lower, upper, frame = (bounds[i] for i in range(3))
    flash_start(state)
    q_s[...] = q_ref[...].T

    def span(at):
        start = jnp.where(at >= upper, upper, jnp.where(at >= lower, lower, 0))
        end = jnp.where(at < lower, lower, jnp.where(at < upper, upper, rows * pieces))
        return start, end

    first_start, first_end = span(frame * rows)
    last_start, last_end = span(frame * rows + rows - 1)

    def piece(d, _):
        base = d * rows

        def attend(masked):
            row_at = pl.multiple_of(d * 2 * VIT_HDIM, 2 * VIT_HDIM)
            key_t = kv_ref[pl.ds(row_at, VIT_HDIM), :]
            value = kv_ref[pl.ds(row_at + VIT_HDIM, VIT_HDIM), :].T
            allowed = None
            if masked:
                at = frame * rows + lax.broadcasted_iota(jnp.int32, (rows, 1), 0)
                start, end = span(at)
                key_at = base + lax.broadcasted_iota(jnp.int32, (1, rows), 1)
                allowed = (key_at >= start) & (key_at < end)
            flash_block(q_s[...], key_t, value, 0, 0, state, VIT_HDIM**-0.5 * log2e, allowed)

        live = (base < last_end) & (base + rows > first_start)
        whole = (base >= last_start) & (base + rows <= first_end)
        pl.when(live & whole)(lambda: attend(False))
        pl.when(live & jnp.logical_not(whole))(lambda: attend(True))
        return 0

    lax.fori_loop(0, pieces, piece, 0)
    out_ref[...] = flash_end(state).T.astype(bf16)


def vit_attention(bounds, query_t, pairs):
    width, rows = query_t.shape
    whole = pl.BlockSpec(memory_space=pltpu.VMEM)
    return pl.pallas_call(
        vit_kernel,
        out_shape=jax.ShapeDtypeStruct((width, rows), bf16),
        in_specs=[pl.BlockSpec(memory_space=pltpu.SMEM), whole, whole],
        out_specs=whole,
        scratch_shapes=[pltpu.VMEM((rows, width), bf16)]
        + [pltpu.VMEM(s, f32) for s in ((rows, HDIM), (rows, HDIM), (rows, width))],
        compiler_params=pltpu.CompilerParams(vmem_limit_bytes=vmem_limit),
        cost_estimate=pl.CostEstimate(
            flops=32 * rows * rows * width * 2, bytes_accessed=4 * rows * rows, transcendentals=0
        ),
    )(bounds, query_t, pairs)


def merger_kernel(place, ctx, *refs, rows, side):
    out_w, refs = refs[:CORES], refs[CORES:]
    patches, gain, up, down, sel_z, sel_y = refs[:6]
    parts = refs[6 : 6 + 2 * side]
    proj, up_v, down_v, normed, sems = refs[6 + 2 * side :]
    y_at, z_at, head = place[0], place[1], VIT_HDIM
    copies = []
    for i in range(side):
        for j in range(side):
            at = (((y_at - i + side) % side) * side + (z_at - j + side) % side) * head
            rows_at = pl.ds(pl.multiple_of(at, head), head)
            for c, source in enumerate(out_w):
                wide = source.shape[1]
                columns = pl.multiple_of(((place[2] + c) % CORES) * wide, wide)
                copies.append(
                    (
                        source.at[pl.ds((i * side + j) * head, head), :],
                        proj.at[rows_at, pl.ds(columns, wide)],
                    )
                )
    copies += [(up, up_v), (down, down_v)]
    started = [pltpu.make_async_copy(a, b, sems.at[i]) for i, (a, b) in enumerate(copies)]
    for c in started:
        c.start()
    for c in started[:-2]:
        c.wait()
    out = patches[...].astype(f32) + dot(ctx[...], proj[...], ((0,), (0,)))
    factor = lax.rsqrt(jnp.mean(out * out, axis=1, keepdims=True) + epsilon)
    for b in range(normed.shape[0]):
        lane = slice(b * HDIM, (b + 1) * HDIM)
        normed[b] = out[:, lane] * factor * gain[:, lane]
    started[-2].wait()
    tokens, width = rows // 4, proj.shape[1]
    hidden = jnp.zeros((tokens, up_v.shape[0]), f32)
    for r in range(4):
        line = jnp.concatenate(
            [
                normed[b, pl.ds(r, tokens, stride=4), :].astype(bf16)
                for b in range(normed.shape[0])
            ],
            axis=1,
        )
        hidden = hidden + dot(line, up_v[:, r * width : (r + 1) * width], ((1,), (1,)))
    hidden = (0.5 * hidden * (1.0 + lax.erf(hidden * math.sqrt(0.5)))).astype(bf16)
    started[-1].wait()
    columns = down_v.shape[1] // 2
    block = math.gcd(columns, 1024)
    taken = sel_z.shape[0] // side
    for n, sel in enumerate((sel_z, sel_y)):
        mine = dot(sel[...], hidden).astype(bf16)
        for b in range(columns // block):
            at = n * columns + b * block
            sums = dot(mine, down_v[:, at : at + block])
            for d in range(side):
                parts[n * side + d][:, b * block : (b + 1) * block] = sums[
                    d * taken : (d + 1) * taken, :
                ].astype(bf16)


def merger(place, ctx, out_w, patches, gain, up, down, sel_z, sel_y):
    rows, width = patches.shape
    whole, far = pl.BlockSpec(memory_space=pltpu.VMEM), pl.BlockSpec(memory_space=pl.ANY)
    side = SIDE
    taken = sel_z.shape[0] // side
    part = jax.ShapeDtypeStruct((taken, down.shape[1] // 2), bf16)
    return pl.pallas_call(
        functools.partial(merger_kernel, rows=rows, side=side),
        out_shape=[part] * (2 * side),
        in_specs=[pl.BlockSpec(memory_space=pltpu.SMEM), whole]
        + [far] * CORES
        + [whole, whole, far, far, whole, whole],
        out_specs=[whole] * (2 * side),
        scratch_shapes=[
            pltpu.VMEM(ctx.shape[:1] + (width,), bf16),
            pltpu.VMEM(up.shape, bf16),
            pltpu.VMEM(down.shape, bf16),
            pltpu.VMEM((width // HDIM, rows, HDIM), f32),
            pltpu.SemaphoreType.DMA((side * side * CORES + 2,)),
        ],
        compiler_params=pltpu.CompilerParams(vmem_limit_bytes=vmem_limit),
        cost_estimate=pl.CostEstimate(
            flops=2 * rows * width * width * 3, bytes_accessed=20 * 1024 * 1024, transcendentals=0
        ),
    )(place, ctx, *out_w, patches, gain, up, down, sel_z, sel_y)


def project_kernel(*refs, lots, steps, combine):
    xs, (gain, wq, wkv, cos, sin) = refs[:lots], refs[lots : lots + 5]
    refs = refs[lots + 5 :]
    if combine:
        text, where_ref, q_out, kv_out = refs[:4]
    else:
        out_ref = refs[0]
    acc, factor = refs[-2:]
    step = pl.program_id(0)
    width = xs[0].shape[1]
    part = width // steps
    n_query = wq.shape[1]
    bases = [0]
    for x_ref in xs:
        bases.append(bases[-1] + x_ref.shape[0])

    @pl.when(step == 0)
    def _():
        for x_ref, base in zip(xs, bases):
            squares = jnp.zeros((x_ref.shape[0], HDIM), f32)
            for i in range(width // HDIM):
                piece = x_ref[:, i * HDIM : (i + 1) * HDIM].astype(f32)
                squares = squares + piece * piece
            factor[base : base + x_ref.shape[0], :] = lax.rsqrt(
                jnp.sum(squares, axis=1, keepdims=True) / width + epsilon
            )
        acc[...] = jnp.zeros(acc.shape, f32)

    at = pl.multiple_of(step * part, part)
    mine = jnp.concatenate(
        [
            (
                x_ref[:, pl.ds(at, part)].astype(f32)
                * factor[base : base + x_ref.shape[0], :]
                * gain[...]
            ).astype(bf16)
            for x_ref, base in zip(xs, bases)
        ],
        axis=0,
    )
    acc[:, :n_query] += dot(mine, wq[...])
    acc[:, n_query:] += dot(mine, wkv[...])

    @pl.when(step == steps - 1)
    def _():
        heads = n_query // HDIM + 1
        turned = []
        for h in range(heads):
            raw = acc[:, h * HDIM : (h + 1) * HDIM]
            turned.append(
                (raw * cos[...] + pltpu.roll(raw, HDIM // 2, 1) * sin[...]).astype(bf16)
            )
        turned.append(acc[:, heads * HDIM :].astype(bf16))
        done = jnp.concatenate(turned, axis=1)
        if not combine:
            out_ref[...] = done
        else:
            every = jnp.concatenate([text[:, :n_query], done[:, :n_query]], axis=0)
            place = where_ref[...]
            over = ((0,), (0,))
            q_out[...] = dot(place, every, over).astype(bf16)
            kv_out[...] = done[:, n_query:]


def project(xs, gain, wq, wkv, cos, sin, combine=None):
    rows, width = sum(x.shape[0] for x in xs), xs[0].shape[1]
    steps = 8
    part = width // steps
    n_out = wq.shape[1] + wkv.shape[1]

    def full(a):
        return pl.BlockSpec(a.shape, lambda i: (0,) * len(a.shape))

    extra = []
    if combine is None:
        outs = jax.ShapeDtypeStruct((rows, n_out), bf16)
        out_specs = full(outs)
    else:
        extra = list(combine)
        block = combine[1].shape[1]
        outs = [
            jax.ShapeDtypeStruct((block, wq.shape[1]), bf16),
            jax.ShapeDtypeStruct((rows, wkv.shape[1]), bf16),
        ]
        out_specs = [full(o) for o in outs]
    return pl.pallas_call(
        functools.partial(
            project_kernel, lots=len(xs), steps=steps, combine=combine is not None
        ),
        grid=(steps,),
        out_shape=outs,
        in_specs=[full(x) for x in xs]
        + [
            pl.BlockSpec((1, part), lambda i: (0, i)),
            pl.BlockSpec((part, wq.shape[1]), lambda i: (i, 0)),
            pl.BlockSpec((part, wkv.shape[1]), lambda i: (i, 0)),
            full(cos),
            full(sin),
        ]
        + [full(e) for e in extra],
        out_specs=out_specs,
        scratch_shapes=[pltpu.VMEM((rows, n_out), f32), pltpu.VMEM((rows, 1), f32)],
        compiler_params=pltpu.CompilerParams(vmem_limit_bytes=vmem_limit),
        cost_estimate=pl.CostEstimate(
            flops=2 * rows * width * n_out,
            bytes_accessed=2 * width * (rows + n_out),
            transcendentals=0,
        ),
    )(*xs, gain, wq, wkv, cos, sin, *extra)


def llm_kernel(place, q_ref, kv_ref, vision_ref, spot_ref, out_ref, q_s, *state):
    rows, heads = q_ref.shape[0], q_ref.shape[1] // HDIM
    step = 2 * rows
    own = place[0]
    flash_start(state)
    for h in range(heads):
        q_s[h * rows : (h + 1) * rows, :] = q_ref[:, h * HDIM : (h + 1) * HDIM]

    slots = spot_ref.shape[1]

    def joined(b):
        spot = spot_ref[pl.ds(b, 1), :]
        hit = lax.broadcasted_iota(jnp.int32, (rows, slots), 0) == spot
        vision = vision_ref[pl.ds(pl.multiple_of(b * slots, slots), slots), :]
        moved_in = dot(jnp.where(hit, 1.0, 0.0).astype(bf16), vision)
        text = kv_ref[pl.ds(pl.multiple_of(b * rows, rows), rows), :]
        return (text.astype(f32) + moved_in).astype(bf16)

    def block(j, masked):
        allowed = None
        if masked:
            line = lax.broadcasted_iota(jnp.int32, (heads * rows, 1), 0)
            key_at = j * step + lax.broadcasted_iota(jnp.int32, (1, step), 1)
            allowed = key_at <= own * rows + line % rows
        pair = jnp.concatenate([joined(2 * j), joined(2 * j + 1)], axis=0)
        key, value = pair[:, :HDIM], pair[:, HDIM:]
        flash_block(q_s[...], key, value, 1, 0, state, HDIM**-0.5 * log2e, allowed)

    lax.fori_loop(0, own // 2, lambda j, _: block(j, False), None)
    block(own // 2, True)
    result = flash_end(state).astype(bf16)
    for h in range(heads):
        out_ref[:, h * HDIM : (h + 1) * HDIM] = result[h * rows : (h + 1) * rows, :]


def llm_attention(place, query, pairs, vision_pairs, spots):
    rows, width = query.shape
    whole = pl.BlockSpec(memory_space=pltpu.VMEM)
    lines = rows * (width // HDIM)
    return pl.pallas_call(
        llm_kernel,
        out_shape=jax.ShapeDtypeStruct((rows, width), bf16),
        in_specs=[pl.BlockSpec(memory_space=pltpu.SMEM)] + [whole] * 4,
        out_specs=whole,
        scratch_shapes=[pltpu.VMEM((lines, HDIM), bf16)] + [pltpu.VMEM((lines, HDIM), f32)] * 3,
        compiler_params=pltpu.CompilerParams(vmem_limit_bytes=vmem_limit),
        cost_estimate=pl.CostEstimate(
            flops=64 * rows * rows * width, bytes_accessed=2**23, transcendentals=0
        ),
    )(place, query, pairs, vision_pairs, spots)


def rotary_tables(positions):
    half = HDIM // 2
    inverse = rope_base ** (-2.0 * jnp.arange(half, dtype=f32) / HDIM)
    angles = positions.astype(f32)[:, None] * inverse[None, :]
    cosine, sine = jnp.cos(angles), jnp.sin(angles)
    return jnp.concatenate([cosine, cosine], axis=1), jnp.concatenate([-sine, sine], axis=1)


def local(
    patches,
    vit_gain,
    vision_qkv,
    vision_out,
    video_ids,
    merge_gain,
    merge_up,
    merge_down,
    vision_pos,
    text_embed,
    llm_gain,
    query_weight,
    keyvalue_weight,
):
    frame = lax.axis_index("frame").astype(jnp.int32)
    seq = lax.axis_index("seq").astype(jnp.int32)
    y_at, z_at = seq // SIDE, seq % SIDE
    frames, blocks = CORES * SIDE, SIDE * SIDE
    tokens = vision_pos.shape[0] // frames
    seq_block = text_embed.shape[0] * frames
    cap = 3 * tokens // (2 * blocks)
    slot_rows = -(-cap // 8) * 8

    normed = rms_scale(patches, vit_gain).astype(bf16)
    projected = dot(vision_qkv, normed, ((0,), (1,))).astype(bf16)
    vit_query, vit_pairs = projected[:VIT_HDIM], projected[VIT_HDIM:]
    core = frame % CORES
    wide = vision_out.shape[1] // CORES
    half_out = lax.dynamic_slice_in_dim(vision_out, core * wide, wide, 1)
    ring = ring_gather(half_out, "z")
    lines = [moved(ring, "y", d) for d in range(1, SIDE)]
    counts = [4 * jnp.sum((video_ids < v).astype(jnp.int32)) for v in (1, 2)]
    bounds = jnp.stack(counts + [frame]).astype(jnp.int32)
    pos = vision_pos.reshape(frames, tokens)
    owner = pos // seq_block
    earlier = jnp.arange(tokens)[:, None] > jnp.arange(tokens)[None, :]
    rank = jnp.sum(
        ((owner[:, :, None] == owner[:, None, :]) & earlier[None]).astype(jnp.int32), axis=2
    )
    back = (frame // CORES - jnp.arange(SIDE, dtype=jnp.int32)) % SIDE
    order = jnp.concatenate([back * CORES + core, back * CORES + 1 - core])
    pos_in, rank_in = jnp.take(pos, order, axis=0), jnp.take(rank, order, axis=0)
    ready = (bounds, vit_query, pos_in, rank_in)
    lines[:2], ready = lax.optimization_barrier((lines[:2], ready))
    bounds, vit_query, pos_in, rank_in = ready
    pairs = after(lax.all_gather(vit_pairs, "frame", axis=0, tiled=True), lines[:2])
    texts = lax.all_gather(after(text_embed, pairs), "frame", axis=0, tiled=True)
    context_t = vit_attention(bounds, vit_query, pairs)
    out_w = jnp.concatenate([ring] + after(lines, context_t), axis=0)
    out_w = [out_w, moved(out_w, "core", 1)]

    own_owner = lax.dynamic_slice_in_dim(owner, frame, 1, 0)[0]
    own_rank = lax.dynamic_slice_in_dim(rank, frame, 1, 0)[0]
    d_at = jnp.arange(SIDE, dtype=jnp.int32)[:, None]
    e_at = (jnp.arange(SIDE * cap, dtype=jnp.int32) // cap)[None, :]
    slot = (jnp.arange(SIDE * cap, dtype=jnp.int32) % cap)[None, :]

    def selector(to_y, to_z):
        block = (to_y % SIDE) * SIDE + to_z % SIDE
        return (
            (own_owner[None, None, :] == block[:, :, None])
            & (own_rank[None, None, :] == slot[:, :, None])
        ).astype(bf16).reshape(-1, tokens)

    sel_z = selector(y_at + e_at, z_at + d_at)
    sel_y = selector(y_at + d_at, z_at + e_at)

    block_at = jnp.arange(blocks, dtype=jnp.int32)[:, None, None, None]
    in_slot = (pos_in // seq_block == block_at[:, :, :, 0])[:, :, None, :] & (
        rank_in[:, None, :] == jnp.arange(slot_rows, dtype=jnp.int32)[None, :, None]
    )[None]
    within = (pos_in % seq_block + 1)[None, :, None, :]
    spots = (jnp.sum(jnp.where(in_slot, within, 0), axis=3) - 1).reshape(blocks, -1)
    spot = lax.dynamic_slice_in_dim(spots, seq, 1, 0)[0]
    line = jnp.arange(seq_block, dtype=jnp.int32)
    place_vision = spot[:, None] == line[None, :]
    taken_by_text = ~jnp.any(place_vision, axis=0)
    place_text = (line[:, None] == line[None, :]) & taken_by_text[None, :]
    place = jnp.concatenate([place_text, place_vision], axis=0).astype(bf16)

    gain = llm_gain[None, :]
    cos, sin = rotary_tables(seq * seq_block + jnp.concatenate([line, spot]))
    n_text = seq_block
    weights = (query_weight, keyvalue_weight)

    contexts = sent_to_all(context_t)
    parts = merger(
        jnp.stack([y_at, z_at, core]),
        contexts.reshape(-1, patches.shape[0]),
        out_w,
        patches,
        merge_gain[None, :],
        merge_up.T,
        merge_down,
        sel_z,
        sel_y,
    )
    text = project([after(texts, parts)], gain, *weights, cos[:n_text], sin[:n_text])
    text_pair = jnp.where(taken_by_text[:, None], text[:, query_weight.shape[1] :], 0)
    text_pairs = lax.all_gather(text_pair, "seq", axis=0, tiled=True)
    totals = [ring_sum(parts[:SIDE], "z", text_pair), ring_sum(parts[SIDE:], "y", text_pair)]
    rows = []
    for total, second in zip(totals, "yz"):
        total = ring_sum([total[e * cap : (e + 1) * cap] for e in range(SIDE)], second)
        rows.append(jnp.pad(total, ((0, slot_rows - cap), (0, 0))))
    near = ring_gather(jnp.concatenate(rows, axis=1), "x")
    vision = [near, moved(near, "core", 1)]

    query, pair = project(vision, gain, *weights, cos[n_text:], sin[n_text:], (text, place))
    vision_pairs = sent_to_all(pair).reshape(-1, pair.shape[1])
    return llm_attention(seq[None], query, text_pairs, vision_pairs, spots)


def solution(mesh):
    return jax.shard_map(
        local,
        mesh=mesh,
        in_specs=(
            P("frame", None),
            P(),
            P(None, "seq"),
            P("seq", None),
            P(),
            P(),
            P(None, "seq"),
            P("seq", None),
            P(),
            P(("seq", "frame"), None),
            P(),
            P(None, "frame"),
            P(None, "frame"),
        ),
        out_specs=P("seq", "frame"),
        check_vma=False,
    )
```

```python
import functools
import math

import jax
import jax.numpy as jnp
from jax import lax
from jax.experimental import pallas as pl
from jax.experimental.pallas import tpu as pltpu
from jax.sharding import PartitionSpec as P

VIT_HDIM = 80
HDIM = 128
SIDE = 4
CORES = 2

epsilon = 1e-06
rope_base = 1000000.0
lowest = -1e30
log2e = math.log2(math.e)
bf16 = jnp.bfloat16
f32 = jnp.float32
vmem_limit = 56 * 1024 * 1024


def dot(a, b, contract=((1,), (0,))):
    return lax.dot_general(a, b, (contract, ((), ())), preferred_element_type=f32)


def moved(value, way, step):
    if way == "z":
        pairs = [(i, i - i % SIDE + (i + step) % SIDE) for i in range(SIDE * SIDE)]
    elif way == "y":
        pairs = [(i, (i + SIDE * step) % (SIDE * SIDE)) for i in range(SIDE * SIDE)]
    elif way == "x":
        pairs = [(i, (i + CORES * step) % (CORES * SIDE)) for i in range(CORES * SIDE)]
    else:
        pairs = [(i, i ^ 1) for i in range(CORES * SIDE)]
    return lax.ppermute(value, "seq" if way in "zy" else "frame", pairs)


def after(values, *others):
    return lax.optimization_barrier((values, others))[0]


def sent_to_all(value):
    copies = jnp.broadcast_to(value, (SIDE * SIDE, *value.shape))
    return lax.all_to_all(copies, "seq", split_axis=0, concat_axis=0, tiled=True)


def ring_gather(value, way, *others):
    arrived = [moved(value, way, d) for d in range(1, SIDE)]
    if others:
        arrived = after(arrived, *others)
    return jnp.concatenate([value] + arrived, axis=0)


def ring_sum(parts, way, *others):
    arrived = [moved(parts[d], way, d) for d in range(1, SIDE)]
    if others:
        arrived = after(arrived, *others)
    total = parts[0].astype(f32)
    for a in arrived:
        total = total + a.astype(f32)
    return total.astype(bf16)


def rms_scale(matrix, scales):
    widened = matrix.astype(f32)
    factor = lax.rsqrt(jnp.mean(widened * widened, axis=-1, keepdims=True) + epsilon)
    return widened * factor * scales


def flash_block(query, key, value, over_key, over_value, refs, scale, allowed):
    m_ref, l_ref, a_ref = refs
    scores = dot(query, key, ((1,), (over_key,)))
    if allowed is not None:
        scores = jnp.where(allowed, scores, lowest)
    lanes = [slice(i * HDIM, (i + 1) * HDIM) for i in range(scores.shape[1] // HDIM)]
    top = scores[:, lanes[0]]
    for lane in lanes[1:]:
        top = jnp.maximum(top, scores[:, lane])
    old = m_ref[...]
    new = jnp.maximum(old, jnp.max(top, axis=1, keepdims=True))
    shrink = jnp.exp2((old - new) * scale)
    total, weights = l_ref[...] * shrink, []
    for lane in lanes:
        part = jnp.exp2((scores[:, lane] - new) * scale)
        total = total + part
        weights.append(part.astype(bf16))
    mixed = dot(jnp.concatenate(weights, axis=1), value, ((1,), (over_value,)))
    a_ref[...] = a_ref[...] * shrink[:, : mixed.shape[1]] + mixed
    l_ref[...] = total
    m_ref[...] = new


def flash_start(refs):
    refs[0][...] = jnp.full(refs[0].shape, lowest, f32)
    refs[1][...] = jnp.zeros(refs[1].shape, f32)
    refs[2][...] = jnp.zeros(refs[2].shape, f32)


def flash_end(refs):
    return refs[2][...] / jnp.sum(refs[1][...], axis=1, keepdims=True)


def vit_kernel(bounds, q_ref, kv_ref, out_ref, q_s, *state):
    rows = q_ref.shape[1]
    pieces = kv_ref.shape[0] // (2 * VIT_HDIM)
    lower, upper, frame = (bounds[i] for i in range(3))
    flash_start(state)
    q_s[...] = q_ref[...].T

    def span(at):
        start = jnp.where(at >= upper, upper, jnp.where(at >= lower, lower, 0))
        end = jnp.where(at < lower, lower, jnp.where(at < upper, upper, rows * pieces))
        return start, end

    first_start, first_end = span(frame * rows)
    last_start, last_end = span(frame * rows + rows - 1)

    def piece(d, _):
        base = d * rows

        def attend(masked):
            row_at = pl.multiple_of(d * 2 * VIT_HDIM, 2 * VIT_HDIM)
            key_t = kv_ref[pl.ds(row_at, VIT_HDIM), :]
            value = kv_ref[pl.ds(row_at + VIT_HDIM, VIT_HDIM), :].T
            allowed = None
            if masked:
                at = frame * rows + lax.broadcasted_iota(jnp.int32, (rows, 1), 0)
                start, end = span(at)
                key_at = base + lax.broadcasted_iota(jnp.int32, (1, rows), 1)
                allowed = (key_at >= start) & (key_at < end)
            flash_block(q_s[...], key_t, value, 0, 0, state, VIT_HDIM**-0.5 * log2e, allowed)

        live = (base < last_end) & (base + rows > first_start)
        whole = (base >= last_start) & (base + rows <= first_end)
        pl.when(live & whole)(lambda: attend(False))
        pl.when(live & jnp.logical_not(whole))(lambda: attend(True))
        return 0

    lax.fori_loop(0, pieces, piece, 0)
    out_ref[...] = flash_end(state).T.astype(bf16)


def vit_attention(bounds, query_t, pairs):
    width, rows = query_t.shape
    whole = pl.BlockSpec(memory_space=pltpu.VMEM)
    return pl.pallas_call(
        vit_kernel,
        out_shape=jax.ShapeDtypeStruct((width, rows), bf16),
        in_specs=[pl.BlockSpec(memory_space=pltpu.SMEM), whole, whole],
        out_specs=whole,
        scratch_shapes=[pltpu.VMEM((rows, width), bf16)]
        + [pltpu.VMEM(s, f32) for s in ((rows, HDIM), (rows, HDIM), (rows, width))],
        compiler_params=pltpu.CompilerParams(vmem_limit_bytes=vmem_limit),
        cost_estimate=pl.CostEstimate(
            flops=32 * rows * rows * width * 2, bytes_accessed=4 * rows * rows, transcendentals=0
        ),
    )(bounds, query_t, pairs)


def merger_kernel(place, ctx, *refs, rows, side):
    out_w, refs = refs[:CORES], refs[CORES:]
    patches, gain, up, down, sel_z, sel_y = refs[:6]
    parts = refs[6 : 6 + 2 * side]
    proj, up_v, down_v, normed, sems = refs[6 + 2 * side :]
    y_at, z_at, head = place[0], place[1], VIT_HDIM
    copies = []
    for i in range(side):
        for j in range(side):
            at = (((y_at - i + side) % side) * side + (z_at - j + side) % side) * head
            rows_at = pl.ds(pl.multiple_of(at, head), head)
            for c, source in enumerate(out_w):
                wide = source.shape[1]
                columns = pl.multiple_of(((place[2] + c) % CORES) * wide, wide)
                copies.append(
                    (
                        source.at[pl.ds((i * side + j) * head, head), :],
                        proj.at[rows_at, pl.ds(columns, wide)],
                    )
                )
    copies += [(up, up_v), (down, down_v)]
    started = [pltpu.make_async_copy(a, b, sems.at[i]) for i, (a, b) in enumerate(copies)]
    for c in started:
        c.start()
    for c in started[:-2]:
        c.wait()
    out = patches[...].astype(f32) + dot(ctx[...], proj[...], ((0,), (0,)))
    factor = lax.rsqrt(jnp.mean(out * out, axis=1, keepdims=True) + epsilon)
    for b in range(normed.shape[0]):
        lane = slice(b * HDIM, (b + 1) * HDIM)
        normed[b] = out[:, lane] * factor * gain[:, lane]
    started[-2].wait()
    tokens, width = rows // 4, proj.shape[1]
    hidden = jnp.zeros((tokens, up_v.shape[0]), f32)
    for r in range(4):
        line = jnp.concatenate(
            [
                normed[b, pl.ds(r, tokens, stride=4), :].astype(bf16)
                for b in range(normed.shape[0])
            ],
            axis=1,
        )
        hidden = hidden + dot(line, up_v[:, r * width : (r + 1) * width], ((1,), (1,)))
    hidden = (0.5 * hidden * (1.0 + lax.erf(hidden * math.sqrt(0.5)))).astype(bf16)
    started[-1].wait()
    columns = down_v.shape[1] // 2
    block = math.gcd(columns, 1024)
    taken = sel_z.shape[0] // side
    for n, sel in enumerate((sel_z, sel_y)):
        mine = dot(sel[...], hidden).astype(bf16)
        for b in range(columns // block):
            at = n * columns + b * block
            sums = dot(mine, down_v[:, at : at + block])
            for d in range(side):
                parts[n * side + d][:, b * block : (b + 1) * block] = sums[
                    d * taken : (d + 1) * taken, :
                ].astype(bf16)


def merger(place, ctx, out_w, patches, gain, up, down, sel_z, sel_y):
    rows, width = patches.shape
    whole, far = pl.BlockSpec(memory_space=pltpu.VMEM), pl.BlockSpec(memory_space=pl.ANY)
    side = SIDE
    taken = sel_z.shape[0] // side
    part = jax.ShapeDtypeStruct((taken, down.shape[1] // 2), bf16)
    return pl.pallas_call(
        functools.partial(merger_kernel, rows=rows, side=side),
        out_shape=[part] * (2 * side),
        in_specs=[pl.BlockSpec(memory_space=pltpu.SMEM), whole]
        + [far] * CORES
        + [whole, whole, far, far, whole, whole],
        out_specs=[whole] * (2 * side),
        scratch_shapes=[
            pltpu.VMEM(ctx.shape[:1] + (width,), bf16),
            pltpu.VMEM(up.shape, bf16),
            pltpu.VMEM(down.shape, bf16),
            pltpu.VMEM((width // HDIM, rows, HDIM), f32),
            pltpu.SemaphoreType.DMA((side * side * CORES + 2,)),
        ],
        compiler_params=pltpu.CompilerParams(vmem_limit_bytes=vmem_limit),
        cost_estimate=pl.CostEstimate(
            flops=2 * rows * width * width * 3, bytes_accessed=20 * 1024 * 1024, transcendentals=0
        ),
    )(place, ctx, *out_w, patches, gain, up, down, sel_z, sel_y)


def project_kernel(*refs, lots, steps, combine):
    xs, (gain, wq, wkv, cos, sin) = refs[:lots], refs[lots : lots + 5]
    refs = refs[lots + 5 :]
    if combine:
        text, where_ref, q_out, kv_out = refs[:4]
    else:
        out_ref = refs[0]
    acc, factor = refs[-2:]
    step = pl.program_id(0)
    width = xs[0].shape[1]
    part = width // steps
    n_query = wq.shape[1]
    bases = [0]
    for x_ref in xs:
        bases.append(bases[-1] + x_ref.shape[0])

    @pl.when(step == 0)
    def _():
        for x_ref, base in zip(xs, bases):
            squares = jnp.zeros((x_ref.shape[0], HDIM), f32)
            for i in range(width // HDIM):
                piece = x_ref[:, i * HDIM : (i + 1) * HDIM].astype(f32)
                squares = squares + piece * piece
            factor[base : base + x_ref.shape[0], :] = lax.rsqrt(
                jnp.sum(squares, axis=1, keepdims=True) / width + epsilon
            )
        acc[...] = jnp.zeros(acc.shape, f32)

    at = pl.multiple_of(step * part, part)
    mine = jnp.concatenate(
        [
            (
                x_ref[:, pl.ds(at, part)].astype(f32)
                * factor[base : base + x_ref.shape[0], :]
                * gain[...]
            ).astype(bf16)
            for x_ref, base in zip(xs, bases)
        ],
        axis=0,
    )
    acc[:, :n_query] += dot(mine, wq[...])
    acc[:, n_query:] += dot(mine, wkv[...])

    @pl.when(step == steps - 1)
    def _():
        heads = n_query // HDIM + 1
        turned = []
        for h in range(heads):
            raw = acc[:, h * HDIM : (h + 1) * HDIM]
            turned.append(
                (raw * cos[...] + pltpu.roll(raw, HDIM // 2, 1) * sin[...]).astype(bf16)
            )
        turned.append(acc[:, heads * HDIM :].astype(bf16))
        done = jnp.concatenate(turned, axis=1)
        if not combine:
            out_ref[...] = done
        else:
            every = jnp.concatenate([text[:, :n_query], done[:, :n_query]], axis=0)
            place = where_ref[...]
            over = ((0,), (0,))
            q_out[...] = dot(place, every, over).astype(bf16)
            kv_out[...] = done[:, n_query:]


def project(xs, gain, wq, wkv, cos, sin, combine=None):
    rows, width = sum(x.shape[0] for x in xs), xs[0].shape[1]
    steps = 8
    part = width // steps
    n_out = wq.shape[1] + wkv.shape[1]

    def full(a):
        return pl.BlockSpec(a.shape, lambda i: (0,) * len(a.shape))

    extra = []
    if combine is None:
        outs = jax.ShapeDtypeStruct((rows, n_out), bf16)
        out_specs = full(outs)
    else:
        extra = list(combine)
        block = combine[1].shape[1]
        outs = [
            jax.ShapeDtypeStruct((block, wq.shape[1]), bf16),
            jax.ShapeDtypeStruct((rows, wkv.shape[1]), bf16),
        ]
        out_specs = [full(o) for o in outs]
    return pl.pallas_call(
        functools.partial(
            project_kernel, lots=len(xs), steps=steps, combine=combine is not None
        ),
        grid=(steps,),
        out_shape=outs,
        in_specs=[full(x) for x in xs]
        + [
            pl.BlockSpec((1, part), lambda i: (0, i)),
            pl.BlockSpec((part, wq.shape[1]), lambda i: (i, 0)),
            pl.BlockSpec((part, wkv.shape[1]), lambda i: (i, 0)),
            full(cos),
            full(sin),
        ]
        + [full(e) for e in extra],
        out_specs=out_specs,
        scratch_shapes=[pltpu.VMEM((rows, n_out), f32), pltpu.VMEM((rows, 1), f32)],
        compiler_params=pltpu.CompilerParams(vmem_limit_bytes=vmem_limit),
        cost_estimate=pl.CostEstimate(
            flops=2 * rows * width * n_out,
            bytes_accessed=2 * width * (rows + n_out),
            transcendentals=0,
        ),
    )(*xs, gain, wq, wkv, cos, sin, *extra)


def llm_kernel(place, q_ref, kv_ref, vision_ref, spot_ref, out_ref, q_s, *state):
    rows, heads = q_ref.shape[0], q_ref.shape[1] // HDIM
    step = 2 * rows
    own = place[0]
    flash_start(state)
    for h in range(heads):
        q_s[h * rows : (h + 1) * rows, :] = q_ref[:, h * HDIM : (h + 1) * HDIM]

    slots = spot_ref.shape[1]

    def joined(b):
        spot = spot_ref[pl.ds(b, 1), :]
        hit = lax.broadcasted_iota(jnp.int32, (rows, slots), 0) == spot
        vision = vision_ref[pl.ds(pl.multiple_of(b * slots, slots), slots), :]
        moved_in = dot(jnp.where(hit, 1.0, 0.0).astype(bf16), vision)
        text = kv_ref[pl.ds(pl.multiple_of(b * rows, rows), rows), :]
        return (text.astype(f32) + moved_in).astype(bf16)

    def block(j, masked):
        allowed = None
        if masked:
            line = lax.broadcasted_iota(jnp.int32, (heads * rows, 1), 0)
            key_at = j * step + lax.broadcasted_iota(jnp.int32, (1, step), 1)
            allowed = key_at <= own * rows + line % rows
        pair = jnp.concatenate([joined(2 * j), joined(2 * j + 1)], axis=0)
        key, value = pair[:, :HDIM], pair[:, HDIM:]
        flash_block(q_s[...], key, value, 1, 0, state, HDIM**-0.5 * log2e, allowed)

    lax.fori_loop(0, own // 2, lambda j, _: block(j, False), None)
    block(own // 2, True)
    result = flash_end(state).astype(bf16)
    for h in range(heads):
        out_ref[:, h * HDIM : (h + 1) * HDIM] = result[h * rows : (h + 1) * rows, :]


def llm_attention(place, query, pairs, vision_pairs, spots):
    rows, width = query.shape
    whole = pl.BlockSpec(memory_space=pltpu.VMEM)
    lines = rows * (width // HDIM)
    return pl.pallas_call(
        llm_kernel,
        out_shape=jax.ShapeDtypeStruct((rows, width), bf16),
        in_specs=[pl.BlockSpec(memory_space=pltpu.SMEM)] + [whole] * 4,
        out_specs=whole,
        scratch_shapes=[pltpu.VMEM((lines, HDIM), bf16)] + [pltpu.VMEM((lines, HDIM), f32)] * 3,
        compiler_params=pltpu.CompilerParams(vmem_limit_bytes=vmem_limit),
        cost_estimate=pl.CostEstimate(
            flops=64 * rows * rows * width, bytes_accessed=2**23, transcendentals=0
        ),
    )(place, query, pairs, vision_pairs, spots)


def rotary_tables(positions):
    half = HDIM // 2
    inverse = rope_base ** (-2.0 * jnp.arange(half, dtype=f32) / HDIM)
    angles = positions.astype(f32)[:, None] * inverse[None, :]
    cosine, sine = jnp.cos(angles), jnp.sin(angles)
    return jnp.concatenate([cosine, cosine], axis=1), jnp.concatenate([-sine, sine], axis=1)


def local(
    patches,
    vit_gain,
    vision_qkv,
    vision_out,
    video_ids,
    merge_gain,
    merge_up,
    merge_down,
    vision_pos,
    text_embed,
    llm_gain,
    query_weight,
    keyvalue_weight,
):
    frame = lax.axis_index("frame").astype(jnp.int32)
    seq = lax.axis_index("seq").astype(jnp.int32)
    y_at, z_at = seq // SIDE, seq % SIDE
    frames, blocks = CORES * SIDE, SIDE * SIDE
    tokens = vision_pos.shape[0] // frames
    seq_block = text_embed.shape[0] * frames
    cap = 3 * tokens // (2 * blocks)
    slot_rows = -(-cap // 8) * 8

    normed = rms_scale(patches, vit_gain).astype(bf16)
    projected = dot(vision_qkv, normed, ((0,), (1,))).astype(bf16)
    vit_query, vit_pairs = projected[:VIT_HDIM], projected[VIT_HDIM:]
    core = frame % CORES
    wide = vision_out.shape[1] // CORES
    half_out = lax.dynamic_slice_in_dim(vision_out, core * wide, wide, 1)
    ring = ring_gather(half_out, "z")
    lines = [moved(ring, "y", d) for d in range(1, SIDE)]
    counts = [4 * jnp.sum((video_ids < v).astype(jnp.int32)) for v in (1, 2)]
    bounds = jnp.stack(counts + [frame]).astype(jnp.int32)
    pos = vision_pos.reshape(frames, tokens)
    owner = pos // seq_block
    earlier = jnp.arange(tokens)[:, None] > jnp.arange(tokens)[None, :]
    rank = jnp.sum(
        ((owner[:, :, None] == owner[:, None, :]) & earlier[None]).astype(jnp.int32), axis=2
    )
    back = (frame // CORES - jnp.arange(SIDE, dtype=jnp.int32)) % SIDE
    order = jnp.concatenate([back * CORES + core, back * CORES + 1 - core])
    pos_in, rank_in = jnp.take(pos, order, axis=0), jnp.take(rank, order, axis=0)
    ready = (bounds, vit_query, pos_in, rank_in)
    lines[:2], ready = lax.optimization_barrier((lines[:2], ready))
    bounds, vit_query, pos_in, rank_in = ready
    pairs = after(lax.all_gather(vit_pairs, "frame", axis=0, tiled=True), lines[:2])
    texts = lax.all_gather(after(text_embed, pairs), "frame", axis=0, tiled=True)
    context_t = vit_attention(bounds, vit_query, pairs)
    out_w = jnp.concatenate([ring] + after(lines, context_t), axis=0)
    out_w = [out_w, moved(out_w, "core", 1)]

    own_owner = lax.dynamic_slice_in_dim(owner, frame, 1, 0)[0]
    own_rank = lax.dynamic_slice_in_dim(rank, frame, 1, 0)[0]
    d_at = jnp.arange(SIDE, dtype=jnp.int32)[:, None]
    e_at = (jnp.arange(SIDE * cap, dtype=jnp.int32) // cap)[None, :]
    slot = (jnp.arange(SIDE * cap, dtype=jnp.int32) % cap)[None, :]

    def selector(to_y, to_z):
        block = (to_y % SIDE) * SIDE + to_z % SIDE
        return (
            (own_owner[None, None, :] == block[:, :, None])
            & (own_rank[None, None, :] == slot[:, :, None])
        ).astype(bf16).reshape(-1, tokens)

    sel_z = selector(y_at + e_at, z_at + d_at)
    sel_y = selector(y_at + d_at, z_at + e_at)

    block_at = jnp.arange(blocks, dtype=jnp.int32)[:, None, None, None]
    in_slot = (pos_in // seq_block == block_at[:, :, :, 0])[:, :, None, :] & (
        rank_in[:, None, :] == jnp.arange(slot_rows, dtype=jnp.int32)[None, :, None]
    )[None]
    within = (pos_in % seq_block + 1)[None, :, None, :]
    spots = (jnp.sum(jnp.where(in_slot, within, 0), axis=3) - 1).reshape(blocks, -1)
    spot = lax.dynamic_slice_in_dim(spots, seq, 1, 0)[0]
    line = jnp.arange(seq_block, dtype=jnp.int32)
    place_vision = spot[:, None] == line[None, :]
    taken_by_text = ~jnp.any(place_vision, axis=0)
    place_text = (line[:, None] == line[None, :]) & taken_by_text[None, :]
    place = jnp.concatenate([place_text, place_vision], axis=0).astype(bf16)

    gain = llm_gain[None, :]
    cos, sin = rotary_tables(seq * seq_block + jnp.concatenate([line, spot]))
    n_text = seq_block
    weights = (query_weight, keyvalue_weight)

    contexts = sent_to_all(context_t)
    parts = merger(
        jnp.stack([y_at, z_at, core]),
        contexts.reshape(-1, patches.shape[0]),
        out_w,
        patches,
        merge_gain[None, :],
        merge_up.T,
        merge_down,
        sel_z,
        sel_y,
    )
    text = project([after(texts, parts)], gain, *weights, cos[:n_text], sin[:n_text])
    text_pair = jnp.where(taken_by_text[:, None], text[:, query_weight.shape[1] :], 0)
    totals = [ring_sum(parts[:SIDE], "z", text_pair), ring_sum(parts[SIDE:], "y", text_pair)]
    text_pairs = lax.all_gather(after(text_pair, totals), "seq", axis=0, tiled=True)
    rows = []
    for total, second in zip(totals, "yz"):
        total = ring_sum([total[e * cap : (e + 1) * cap] for e in range(SIDE)], second)
        rows.append(jnp.pad(total, ((0, slot_rows - cap), (0, 0))))
    cos, sin = cos[n_text:], sin[n_text:]
    near = ring_gather(jnp.concatenate(rows, axis=1), "x", cos, sin, place)
    vision = [near, moved(near, "core", 1)]

    query, pair = project(vision, gain, *weights, cos, sin, (text, place))
    width = pair.shape[1]
    pair = pair.reshape(frames, slot_rows, width)[:, :cap].reshape(-1, width)
    vision_pairs = sent_to_all(pair).reshape(-1, width)
    spots = spots.reshape(blocks, frames, slot_rows)[:, :, :cap].reshape(blocks, -1)
    return llm_attention(seq[None], query, text_pairs, vision_pairs, spots)


def solution(mesh):
    return jax.shard_map(
        local,
        mesh=mesh,
        in_specs=(
            P("frame", None),
            P(),
            P(None, "seq"),
            P("seq", None),
            P(),
            P(),
            P(None, "seq"),
            P("seq", None),
            P(),
            P(("seq", "frame"), None),
            P(),
            P(None, "frame"),
            P(None, "frame"),
        ),
        out_specs=P("seq", "frame"),
        check_vma=False,
    )
```

```python
import functools
import math

import jax
import jax.numpy as jnp
from jax import lax
from jax.experimental import pallas as pl
from jax.experimental.pallas import tpu as pltpu
from jax.sharding import PartitionSpec as P

VIT_HDIM = 80
HDIM = 128
SIDE = 4
CORES = 2

epsilon = 1e-06
rope_base = 1000000.0
lowest = -1e30
log2e = math.log2(math.e)
bf16 = jnp.bfloat16
f32 = jnp.float32
vmem_limit = 56 * 1024 * 1024


def dot(a, b, contract=((1,), (0,))):
    return lax.dot_general(a, b, (contract, ((), ())), preferred_element_type=f32)


def moved(value, way, step):
    if way == "z":
        pairs = [(i, i - i % SIDE + (i + step) % SIDE) for i in range(SIDE * SIDE)]
    elif way == "y":
        pairs = [(i, (i + SIDE * step) % (SIDE * SIDE)) for i in range(SIDE * SIDE)]
    elif way == "x":
        pairs = [(i, (i + CORES * step) % (CORES * SIDE)) for i in range(CORES * SIDE)]
    else:
        pairs = [(i, i ^ 1) for i in range(CORES * SIDE)]
    return lax.ppermute(value, "seq" if way in "zy" else "frame", pairs)


def after(values, *others):
    return lax.optimization_barrier((values, others))[0]


def sent_to_all(value):
    copies = jnp.broadcast_to(value, (SIDE * SIDE, *value.shape))
    return lax.all_to_all(copies, "seq", split_axis=0, concat_axis=0, tiled=True)


def ring_gather(value, way, *others):
    arrived = [moved(value, way, d) for d in range(1, SIDE)]
    if others:
        arrived = after(arrived, *others)
    return jnp.concatenate([value] + arrived, axis=0)


def ring_sum(parts, way, *others):
    arrived = [moved(parts[d], way, d) for d in range(1, SIDE)]
    if others:
        arrived = after(arrived, *others)
    total = parts[0].astype(f32)
    for a in arrived:
        total = total + a.astype(f32)
    return total.astype(bf16)


def rms_scale(matrix, scales):
    widened = matrix.astype(f32)
    factor = lax.rsqrt(jnp.mean(widened * widened, axis=-1, keepdims=True) + epsilon)
    return widened * factor * scales


def flash_block(query, key, value, over_key, over_value, refs, scale, allowed):
    m_ref, l_ref, a_ref = refs
    scores = dot(query, key, ((1,), (over_key,)))
    if allowed is not None:
        scores = jnp.where(allowed, scores, lowest)
    lanes = [slice(i * HDIM, (i + 1) * HDIM) for i in range(scores.shape[1] // HDIM)]
    top = scores[:, lanes[0]]
    for lane in lanes[1:]:
        top = jnp.maximum(top, scores[:, lane])
    old = m_ref[...]
    new = jnp.maximum(old, jnp.max(top, axis=1, keepdims=True))
    shrink = jnp.exp2((old - new) * scale)
    total, weights = l_ref[...] * shrink, []
    for lane in lanes:
        part = jnp.exp2((scores[:, lane] - new) * scale)
        total = total + part
        weights.append(part.astype(bf16))
    mixed = dot(jnp.concatenate(weights, axis=1), value, ((1,), (over_value,)))
    a_ref[...] = a_ref[...] * shrink[:, : mixed.shape[1]] + mixed
    l_ref[...] = total
    m_ref[...] = new


def flash_start(refs):
    refs[0][...] = jnp.full(refs[0].shape, lowest, f32)
    refs[1][...] = jnp.zeros(refs[1].shape, f32)
    refs[2][...] = jnp.zeros(refs[2].shape, f32)


def flash_end(refs):
    return refs[2][...] / jnp.sum(refs[1][...], axis=1, keepdims=True)


def vit_kernel(bounds, q_ref, kv_ref, out_ref, q_s, *state):
    rows = q_ref.shape[1]
    pieces = kv_ref.shape[0] // (2 * VIT_HDIM)
    lower, upper, frame = (bounds[i] for i in range(3))
    flash_start(state)
    q_s[...] = q_ref[...].T

    def span(at):
        start = jnp.where(at >= upper, upper, jnp.where(at >= lower, lower, 0))
        end = jnp.where(at < lower, lower, jnp.where(at < upper, upper, rows * pieces))
        return start, end

    first_start, first_end = span(frame * rows)
    last_start, last_end = span(frame * rows + rows - 1)

    def piece(d, _):
        base = d * rows

        def attend(masked):
            row_at = pl.multiple_of(d * 2 * VIT_HDIM, 2 * VIT_HDIM)
            key_t = kv_ref[pl.ds(row_at, VIT_HDIM), :]
            value = kv_ref[pl.ds(row_at + VIT_HDIM, VIT_HDIM), :].T
            allowed = None
            if masked:
                at = frame * rows + lax.broadcasted_iota(jnp.int32, (rows, 1), 0)
                start, end = span(at)
                key_at = base + lax.broadcasted_iota(jnp.int32, (1, rows), 1)
                allowed = (key_at >= start) & (key_at < end)
            flash_block(q_s[...], key_t, value, 0, 0, state, VIT_HDIM**-0.5 * log2e, allowed)

        live = (base < last_end) & (base + rows > first_start)
        whole = (base >= last_start) & (base + rows <= first_end)
        pl.when(live & whole)(lambda: attend(False))
        pl.when(live & jnp.logical_not(whole))(lambda: attend(True))
        return 0

    lax.fori_loop(0, pieces, piece, 0)
    out_ref[...] = flash_end(state).T.astype(bf16)


def vit_attention(bounds, query_t, pairs):
    width, rows = query_t.shape
    whole = pl.BlockSpec(memory_space=pltpu.VMEM)
    return pl.pallas_call(
        vit_kernel,
        out_shape=jax.ShapeDtypeStruct((width, rows), bf16),
        in_specs=[pl.BlockSpec(memory_space=pltpu.SMEM), whole, whole],
        out_specs=whole,
        scratch_shapes=[pltpu.VMEM((rows, width), bf16)]
        + [pltpu.VMEM(s, f32) for s in ((rows, HDIM), (rows, HDIM), (rows, width))],
        compiler_params=pltpu.CompilerParams(vmem_limit_bytes=vmem_limit),
        cost_estimate=pl.CostEstimate(
            flops=32 * rows * rows * width * 2, bytes_accessed=4 * rows * rows, transcendentals=0
        ),
    )(bounds, query_t, pairs)


def merger_kernel(place, ctx, *refs, rows, side):
    out_w, refs = refs[:CORES], refs[CORES:]
    patches, gain, up, down, sel_z, sel_y = refs[:6]
    parts = refs[6 : 6 + 2 * side]
    proj, up_v, down_v, normed, sems = refs[6 + 2 * side :]
    y_at, z_at, head = place[0], place[1], VIT_HDIM
    copies = []
    for i in range(side):
        for j in range(side):
            at = (((y_at - i + side) % side) * side + (z_at - j + side) % side) * head
            rows_at = pl.ds(pl.multiple_of(at, head), head)
            for c, source in enumerate(out_w):
                wide = source.shape[1]
                columns = pl.multiple_of(((place[2] + c) % CORES) * wide, wide)
                copies.append(
                    (
                        source.at[pl.ds((i * side + j) * head, head), :],
                        proj.at[rows_at, pl.ds(columns, wide)],
                    )
                )
    copies += [(up, up_v), (down, down_v)]
    started = [pltpu.make_async_copy(a, b, sems.at[i]) for i, (a, b) in enumerate(copies)]
    for c in started:
        c.start()
    for c in started[:-2]:
        c.wait()
    out = patches[...].astype(f32) + dot(ctx[...], proj[...], ((0,), (0,)))
    factor = lax.rsqrt(jnp.mean(out * out, axis=1, keepdims=True) + epsilon)
    for b in range(normed.shape[0]):
        lane = slice(b * HDIM, (b + 1) * HDIM)
        normed[b] = out[:, lane] * factor * gain[:, lane]
    started[-2].wait()
    tokens, width = rows // 4, proj.shape[1]
    hidden = jnp.zeros((tokens, up_v.shape[0]), f32)
    for r in range(4):
        line = jnp.concatenate(
            [
                normed[b, pl.ds(r, tokens, stride=4), :].astype(bf16)
                for b in range(normed.shape[0])
            ],
            axis=1,
        )
        hidden = hidden + dot(line, up_v[:, r * width : (r + 1) * width], ((1,), (1,)))
    hidden = (0.5 * hidden * (1.0 + lax.erf(hidden * math.sqrt(0.5)))).astype(bf16)
    started[-1].wait()
    columns = down_v.shape[1] // 2
    block = math.gcd(columns, 1024)
    taken = sel_z.shape[0] // side
    for n, sel in enumerate((sel_z, sel_y)):
        mine = dot(sel[...], hidden).astype(bf16)
        for b in range(columns // block):
            at = n * columns + b * block
            sums = dot(mine, down_v[:, at : at + block])
            for d in range(side):
                parts[n * side + d][:, b * block : (b + 1) * block] = sums[
                    d * taken : (d + 1) * taken, :
                ].astype(bf16)


def merger(place, ctx, out_w, patches, gain, up, down, sel_z, sel_y):
    rows, width = patches.shape
    whole, far = pl.BlockSpec(memory_space=pltpu.VMEM), pl.BlockSpec(memory_space=pl.ANY)
    side = SIDE
    taken = sel_z.shape[0] // side
    part = jax.ShapeDtypeStruct((taken, down.shape[1] // 2), bf16)
    return pl.pallas_call(
        functools.partial(merger_kernel, rows=rows, side=side),
        out_shape=[part] * (2 * side),
        in_specs=[pl.BlockSpec(memory_space=pltpu.SMEM), whole]
        + [far] * CORES
        + [whole, whole, far, far, whole, whole],
        out_specs=[whole] * (2 * side),
        scratch_shapes=[
            pltpu.VMEM(ctx.shape[:1] + (width,), bf16),
            pltpu.VMEM(up.shape, bf16),
            pltpu.VMEM(down.shape, bf16),
            pltpu.VMEM((width // HDIM, rows, HDIM), f32),
            pltpu.SemaphoreType.DMA((side * side * CORES + 2,)),
        ],
        compiler_params=pltpu.CompilerParams(vmem_limit_bytes=vmem_limit),
        cost_estimate=pl.CostEstimate(
            flops=2 * rows * width * width * 3, bytes_accessed=20 * 1024 * 1024, transcendentals=0
        ),
    )(place, ctx, *out_w, patches, gain, up, down, sel_z, sel_y)


def project_kernel(*refs, lots, steps, combine):
    xs, (gain, wq, wkv, cos, sin) = refs[:lots], refs[lots : lots + 5]
    refs = refs[lots + 5 :]
    if combine:
        text, where_ref, q_out, kv_out = refs[:4]
    else:
        out_ref = refs[0]
    acc, factor = refs[-2:]
    step = pl.program_id(0)
    width = xs[0].shape[1]
    part = width // steps
    n_query = wq.shape[1]
    bases = [0]
    for x_ref in xs:
        bases.append(bases[-1] + x_ref.shape[0])

    @pl.when(step == 0)
    def _():
        for x_ref, base in zip(xs, bases):
            squares = jnp.zeros((x_ref.shape[0], HDIM), f32)
            for i in range(width // HDIM):
                piece = x_ref[:, i * HDIM : (i + 1) * HDIM].astype(f32)
                squares = squares + piece * piece
            factor[base : base + x_ref.shape[0], :] = lax.rsqrt(
                jnp.sum(squares, axis=1, keepdims=True) / width + epsilon
            )
        acc[...] = jnp.zeros(acc.shape, f32)

    at = pl.multiple_of(step * part, part)
    mine = jnp.concatenate(
        [
            (
                x_ref[:, pl.ds(at, part)].astype(f32)
                * factor[base : base + x_ref.shape[0], :]
                * gain[...]
            ).astype(bf16)
            for x_ref, base in zip(xs, bases)
        ],
        axis=0,
    )
    acc[:, :n_query] += dot(mine, wq[...])
    acc[:, n_query:] += dot(mine, wkv[...])

    @pl.when(step == steps - 1)
    def _():
        heads = n_query // HDIM + 1
        turned = []
        for h in range(heads):
            raw = acc[:, h * HDIM : (h + 1) * HDIM]
            turned.append(
                (raw * cos[...] + pltpu.roll(raw, HDIM // 2, 1) * sin[...]).astype(bf16)
            )
        turned.append(acc[:, heads * HDIM :].astype(bf16))
        done = jnp.concatenate(turned, axis=1)
        if not combine:
            out_ref[...] = done
        else:
            every = jnp.concatenate([text[:, :n_query], done[:, :n_query]], axis=0)
            place = where_ref[...]
            over = ((0,), (0,))
            q_out[...] = dot(place, every, over).astype(bf16)
            kv_out[...] = done[:, n_query:]


def project(xs, gain, wq, wkv, cos, sin, combine=None):
    rows, width = sum(x.shape[0] for x in xs), xs[0].shape[1]
    steps = 4
    part = width // steps
    n_out = wq.shape[1] + wkv.shape[1]

    def full(a):
        return pl.BlockSpec(a.shape, lambda i: (0,) * len(a.shape))

    extra = []
    if combine is None:
        outs = jax.ShapeDtypeStruct((rows, n_out), bf16)
        out_specs = full(outs)
    else:
        extra = list(combine)
        block = combine[1].shape[1]
        outs = [
            jax.ShapeDtypeStruct((block, wq.shape[1]), bf16),
            jax.ShapeDtypeStruct((rows, wkv.shape[1]), bf16),
        ]
        out_specs = [full(o) for o in outs]
    return pl.pallas_call(
        functools.partial(
            project_kernel, lots=len(xs), steps=steps, combine=combine is not None
        ),
        grid=(steps,),
        out_shape=outs,
        in_specs=[full(x) for x in xs]
        + [
            pl.BlockSpec((1, part), lambda i: (0, i)),
            pl.BlockSpec((part, wq.shape[1]), lambda i: (i, 0)),
            pl.BlockSpec((part, wkv.shape[1]), lambda i: (i, 0)),
            full(cos),
            full(sin),
        ]
        + [full(e) for e in extra],
        out_specs=out_specs,
        scratch_shapes=[pltpu.VMEM((rows, n_out), f32), pltpu.VMEM((rows, 1), f32)],
        compiler_params=pltpu.CompilerParams(vmem_limit_bytes=vmem_limit),
        cost_estimate=pl.CostEstimate(
            flops=2 * rows * width * n_out,
            bytes_accessed=2 * width * (rows + n_out),
            transcendentals=0,
        ),
    )(*xs, gain, wq, wkv, cos, sin, *extra)


def llm_kernel(place, q_ref, kv_ref, vision_ref, spot_ref, out_ref, q_s, *state):
    rows, heads = q_ref.shape[0], q_ref.shape[1] // HDIM
    step = 2 * rows
    own = place[0]
    flash_start(state)
    for h in range(heads):
        q_s[h * rows : (h + 1) * rows, :] = q_ref[:, h * HDIM : (h + 1) * HDIM]

    slots = spot_ref.shape[1]

    def joined(b):
        spot = spot_ref[pl.ds(b, 1), :]
        hit = lax.broadcasted_iota(jnp.int32, (rows, slots), 0) == spot
        vision = vision_ref[pl.ds(pl.multiple_of(b * slots, slots), slots), :]
        moved_in = dot(jnp.where(hit, 1.0, 0.0).astype(bf16), vision)
        text = kv_ref[pl.ds(pl.multiple_of(b * rows, rows), rows), :]
        return (text.astype(f32) + moved_in).astype(bf16)

    def block(j, masked):
        allowed = None
        if masked:
            line = lax.broadcasted_iota(jnp.int32, (heads * rows, 1), 0)
            key_at = j * step + lax.broadcasted_iota(jnp.int32, (1, step), 1)
            allowed = key_at <= own * rows + line % rows
        pair = jnp.concatenate([joined(2 * j), joined(2 * j + 1)], axis=0)
        key, value = pair[:, :HDIM], pair[:, HDIM:]
        flash_block(q_s[...], key, value, 1, 0, state, HDIM**-0.5 * log2e, allowed)

    lax.fori_loop(0, own // 2, lambda j, _: block(j, False), None)
    block(own // 2, True)
    result = flash_end(state).astype(bf16)
    for h in range(heads):
        out_ref[:, h * HDIM : (h + 1) * HDIM] = result[h * rows : (h + 1) * rows, :]


def llm_attention(place, query, pairs, vision_pairs, spots):
    rows, width = query.shape
    whole = pl.BlockSpec(memory_space=pltpu.VMEM)
    lines = rows * (width // HDIM)
    return pl.pallas_call(
        llm_kernel,
        out_shape=jax.ShapeDtypeStruct((rows, width), bf16),
        in_specs=[pl.BlockSpec(memory_space=pltpu.SMEM)] + [whole] * 4,
        out_specs=whole,
        scratch_shapes=[pltpu.VMEM((lines, HDIM), bf16)] + [pltpu.VMEM((lines, HDIM), f32)] * 3,
        compiler_params=pltpu.CompilerParams(vmem_limit_bytes=vmem_limit),
        cost_estimate=pl.CostEstimate(
            flops=64 * rows * rows * width, bytes_accessed=2**23, transcendentals=0
        ),
    )(place, query, pairs, vision_pairs, spots)


def rotary_tables(positions):
    half = HDIM // 2
    inverse = rope_base ** (-2.0 * jnp.arange(half, dtype=f32) / HDIM)
    angles = positions.astype(f32)[:, None] * inverse[None, :]
    cosine, sine = jnp.cos(angles), jnp.sin(angles)
    return jnp.concatenate([cosine, cosine], axis=1), jnp.concatenate([-sine, sine], axis=1)


def local(
    patches,
    vit_gain,
    vision_qkv,
    vision_out,
    video_ids,
    merge_gain,
    merge_up,
    merge_down,
    vision_pos,
    text_embed,
    llm_gain,
    query_weight,
    keyvalue_weight,
):
    frame = lax.axis_index("frame").astype(jnp.int32)
    seq = lax.axis_index("seq").astype(jnp.int32)
    y_at, z_at = seq // SIDE, seq % SIDE
    frames, blocks = CORES * SIDE, SIDE * SIDE
    tokens = vision_pos.shape[0] // frames
    seq_block = text_embed.shape[0] * frames
    cap = 3 * tokens // (2 * blocks)
    slot_rows = -(-cap // 8) * 8

    normed = rms_scale(patches, vit_gain).astype(bf16)
    projected = dot(vision_qkv, normed, ((0,), (1,))).astype(bf16)
    vit_query, vit_pairs = projected[:VIT_HDIM], projected[VIT_HDIM:]
    core = frame % CORES
    wide = vision_out.shape[1] // CORES
    half_out = lax.dynamic_slice_in_dim(vision_out, core * wide, wide, 1)
    ring = ring_gather(half_out, "z")
    lines = [moved(ring, "y", d) for d in range(1, SIDE)]
    counts = [4 * jnp.sum((video_ids < v).astype(jnp.int32)) for v in (1, 2)]
    bounds = jnp.stack(counts + [frame]).astype(jnp.int32)
    pos = vision_pos.reshape(frames, tokens)
    owner = pos // seq_block
    earlier = jnp.arange(tokens)[:, None] > jnp.arange(tokens)[None, :]
    rank = jnp.sum(
        ((owner[:, :, None] == owner[:, None, :]) & earlier[None]).astype(jnp.int32), axis=2
    )
    back = (frame // CORES - jnp.arange(SIDE, dtype=jnp.int32)) % SIDE
    order = jnp.concatenate([back * CORES + core, back * CORES + 1 - core])
    pos_in, rank_in = jnp.take(pos, order, axis=0), jnp.take(rank, order, axis=0)
    ready = (bounds, vit_query, pos_in, rank_in)
    lines[:2], ready = lax.optimization_barrier((lines[:2], ready))
    bounds, vit_query, pos_in, rank_in = ready
    pairs = after(lax.all_gather(vit_pairs, "frame", axis=0, tiled=True), lines[:2])
    texts = lax.all_gather(after(text_embed, pairs), "frame", axis=0, tiled=True)
    context_t = vit_attention(bounds, vit_query, pairs)
    out_w = jnp.concatenate([ring] + after(lines, context_t), axis=0)
    out_w = [out_w, moved(out_w, "core", 1)]

    own_owner = lax.dynamic_slice_in_dim(owner, frame, 1, 0)[0]
    own_rank = lax.dynamic_slice_in_dim(rank, frame, 1, 0)[0]
    d_at = jnp.arange(SIDE, dtype=jnp.int32)[:, None]
    e_at = (jnp.arange(SIDE * cap, dtype=jnp.int32) // cap)[None, :]
    slot = (jnp.arange(SIDE * cap, dtype=jnp.int32) % cap)[None, :]

    def selector(to_y, to_z):
        block = (to_y % SIDE) * SIDE + to_z % SIDE
        return (
            (own_owner[None, None, :] == block[:, :, None])
            & (own_rank[None, None, :] == slot[:, :, None])
        ).astype(bf16).reshape(-1, tokens)

    sel_z = selector(y_at + e_at, z_at + d_at)
    sel_y = selector(y_at + d_at, z_at + e_at)

    block_at = jnp.arange(blocks, dtype=jnp.int32)[:, None, None, None]
    in_slot = (pos_in // seq_block == block_at[:, :, :, 0])[:, :, None, :] & (
        rank_in[:, None, :] == jnp.arange(slot_rows, dtype=jnp.int32)[None, :, None]
    )[None]
    within = (pos_in % seq_block + 1)[None, :, None, :]
    spots = (jnp.sum(jnp.where(in_slot, within, 0), axis=3) - 1).reshape(blocks, -1)
    spot = lax.dynamic_slice_in_dim(spots, seq, 1, 0)[0]
    line = jnp.arange(seq_block, dtype=jnp.int32)
    place_vision = spot[:, None] == line[None, :]
    taken_by_text = ~jnp.any(place_vision, axis=0)
    place_text = (line[:, None] == line[None, :]) & taken_by_text[None, :]
    place = jnp.concatenate([place_text, place_vision], axis=0).astype(bf16)

    gain = llm_gain[None, :]
    cos, sin = rotary_tables(seq * seq_block + jnp.concatenate([line, spot]))
    n_text = seq_block
    weights = (query_weight, keyvalue_weight)

    contexts = sent_to_all(context_t)
    parts = merger(
        jnp.stack([y_at, z_at, core]),
        contexts.reshape(-1, patches.shape[0]),
        out_w,
        patches,
        merge_gain[None, :],
        merge_up.T,
        merge_down,
        sel_z,
        sel_y,
    )
    text = project([after(texts, parts)], gain, *weights, cos[:n_text], sin[:n_text])
    text_pair = jnp.where(taken_by_text[:, None], text[:, query_weight.shape[1] :], 0)
    totals = [ring_sum(parts[:SIDE], "z", text_pair), ring_sum(parts[SIDE:], "y", text_pair)]
    text_pairs = lax.all_gather(after(text_pair, totals), "seq", axis=0, tiled=True)
    rows = []
    for total, second in zip(totals, "yz"):
        total = ring_sum([total[e * cap : (e + 1) * cap] for e in range(SIDE)], second)
        rows.append(jnp.pad(total, ((0, slot_rows - cap), (0, 0))))
    cos, sin = cos[n_text:], sin[n_text:]
    near = ring_gather(jnp.concatenate(rows, axis=1), "x", cos, sin, place)
    vision = [near, moved(near, "core", 1)]

    query, pair = project(vision, gain, *weights, cos, sin, (text, place))
    width = pair.shape[1]
    pair = pair.reshape(frames, slot_rows, width)[:, :cap].reshape(-1, width)
    vision_pairs = sent_to_all(pair).reshape(-1, width)
    spots = spots.reshape(blocks, frames, slot_rows)[:, :, :cap].reshape(blocks, -1)
    return llm_attention(seq[None], query, text_pairs, vision_pairs, spots)


def solution(mesh):
    return jax.shard_map(
        local,
        mesh=mesh,
        in_specs=(
            P("frame", None),
            P(),
            P(None, "seq"),
            P("seq", None),
            P(),
            P(),
            P(None, "seq"),
            P("seq", None),
            P(),
            P(("seq", "frame"), None),
            P(),
            P(None, "frame"),
            P(None, "frame"),
        ),
        out_specs=P("seq", "frame"),
        check_vma=False,
    )
```
